32 devices in a mesh: ctx: 16 (over z, y, x), pp: 2 (over core).
Axes of the slice: x: 2, y: 2, z: 4, core: 2. Of those that a mesh axis runs over, the one named last changes fastest.
Arguments:
- inputs: bfloat16 [2, 2, 1024, 2048], P('pp', None, 'ctx'), may hold values from -6 to 6
- saved_keys: bfloat16 [2, 2, 1024, 512], P('pp', None, 'ctx'), may hold values from -6 to 6
- saved_values: bfloat16 [2, 2, 1024, 512], P('pp', None, 'ctx'), may hold values from -5 to 5
- query_gain: float32 [2, 2048], P('pp'), may hold values from 0.25 to 1.75
- first_grads: bfloat16 [2, 1024, 2048], P('pp', 'ctx'), may hold values from -5 to 5
- head_grads: bfloat16 [1, 1024, 2048], P(None, 'ctx'), may hold values from -5 to 5
- window: int32 [2, 4], P('pp'), may hold values from 1 to 7, as said below
- stride: int32 [2, 4], P('pp'), may hold values from 16 to 32, as said below
Outputs:
- grads_out: bfloat16 [2, 2, 1024, 2048], P('pp', None, 'ctx')
- key_grads: bfloat16 [2, 2, 1024, 512], P('pp', None, 'ctx')
- value_grads: bfloat16 [2, 2, 1024, 512], P('pp', None, 'ctx')
The draws below stay inside these ranges and needn't reach their ends.
Inputs may be any that keep to these rules, and one draw needn't show every extreme that they name: `window`: every entry is 1 to 7; some entry equals 7 and some equals 1. `stride`: every entry is 16 or 32; both occur.
All inputs are finite; a program needn't handle non-finite values.
Results may differ from the reference program's by a relative error of at most 0.014.
Values may be sent and summed in bfloat16 or wider, within the bound.
A program may use at most 64 MiB of HBM per device.

```python
import jax
import jax.numpy as jnp
from jax import lax

BLK = 64
WIN = 7
STRIDE = 16
TICKS = 2
KV_HEADS = 4
HEAD_DIM = 128
GROUP = 4
FEAT = 2048
KVW = 512
SEQ = 1024
SUMMARY = 1
LAYERS = 2
N_CTX = 16


def draw_inputs(key, part):
    key = jax.random.fold_in(key, 11)
    base = jnp.clip(jax.random.normal(key, (LAYERS, TICKS, SEQ, FEAT), jnp.float32), -4.0, 4.0)
    return base.astype(jnp.bfloat16)


def draw_saved_keys(key, part):
    key = jax.random.fold_in(key, 12)
    base = jnp.clip(jax.random.normal(key, (LAYERS, TICKS, SEQ, KVW), jnp.float32), -4.0, 4.0)
    return base.astype(jnp.bfloat16)


def draw_window(key, part):
    key = jax.random.fold_in(key, 13)
    values = jax.random.randint(key, (LAYERS * KV_HEADS,), 1, WIN + 1)
    order = jax.random.permutation(jax.random.fold_in(key, 1), LAYERS * KV_HEADS)
    values = values.at[order[0]].set(WIN).at[order[1]].set(1)
    return values.reshape(LAYERS, KV_HEADS).astype(jnp.int32)


def draw_stride(key, part):
    key = jax.random.fold_in(key, 14)
    values = STRIDE * (1 + jax.random.randint(key, (LAYERS * KV_HEADS,), 0, 2))
    order = jax.random.permutation(jax.random.fold_in(key, 1), LAYERS * KV_HEADS)
    values = values.at[order[0]].set(STRIDE).at[order[1]].set(2 * STRIDE)
    return values.reshape(LAYERS, KV_HEADS).astype(jnp.int32)


def block_levels(rng, shape, split, low, top_value):
    level = 1.0
    for axis_at, shards_of in split:
        heights = jax.random.uniform(jax.random.fold_in(jax.random.fold_in(rng, 6), axis_at), (shards_of,), jnp.float32, low / len(split), top_value / len(split))
        level = level * jnp.repeat(jnp.exp(heights), shape[axis_at] // shards_of).reshape((-1,) + (1,) * (len(shape) - 1 - axis_at))
    return level


def normal_values(rng, shape, deviation, reach, shards=(), held_as=jnp.bfloat16):
    loudness = block_levels(rng, shape, shards, -0.22, 0.18) if shards else 1.0
    values = jax.random.normal(rng, shape, jnp.float32) * deviation * loudness
    return jnp.minimum(jnp.maximum(values, -reach), reach).astype(held_as)


def setup_inputs(seed: int = 0) -> dict:
    streams_of = jax.random.split(jax.random.key(seed), 9)
    return {
        "inputs": draw_inputs(jax.random.fold_in(streams_of[8], 71), 0),
        "saved_keys": draw_saved_keys(jax.random.fold_in(streams_of[8], 71), 0),
        "saved_values": normal_values(streams_of[2], (LAYERS, TICKS, SEQ, KVW), 1.0, 5.0, ((0, 2), (2, 16))),
        "query_gain": jnp.clip(1.0 + 0.15 * jax.random.normal(streams_of[3], (LAYERS, FEAT), jnp.float32), 0.25, 1.75),
        "first_grads": normal_values(streams_of[4], (LAYERS, SEQ, FEAT), 1.0, 5.0, ((0, 2), (1, 16))),
        "head_grads": normal_values(streams_of[5], (TICKS - 1, SEQ, FEAT), 1.0, 5.0, ((1, 16),)),
        "window": draw_window(jax.random.fold_in(streams_of[8], 71), 0),
        "stride": draw_stride(jax.random.fold_in(streams_of[8], 71), 0),
    }


def block_allowed(block, window, stride, summary_count):
    row_ids = jnp.arange(BLK, dtype=jnp.int32)
    query_pos = block * BLK + row_ids
    col_ids = jnp.arange(WIN * BLK, dtype=jnp.int32)
    key_block = block - WIN + 1 + col_ids // BLK
    key_pos = (block - WIN + 1) * BLK + col_ids
    local_ok = (key_block[None, None, :] >= 0) & (key_pos[None, None, :] <= query_pos[None, :, None])
    local_ok = local_ok & ((block - key_block)[None, None, :] < window[:, None, None])
    strided_block = STRIDE * (jnp.arange(summary_count * BLK, dtype=jnp.int32) // BLK)
    strided_ok = (strided_block[None, None, :] % stride[:, None, None] == 0)
    strided_ok = strided_ok & (strided_block[None, None, :] <= block - window[:, None, None])
    heads = window.shape[0]
    local_ok = jnp.broadcast_to(local_ok, (heads, BLK, WIN * BLK))
    strided_ok = jnp.broadcast_to(strided_ok, (heads, BLK, summary_count * BLK))
    return jnp.concatenate([local_ok, strided_ok], axis=2)


def layer_backward(inputs, saved_keys, saved_values, gain, grad_out, window, stride):
    scale = HEAD_DIM ** -0.5
    queries = (inputs.astype(jnp.float32) * gain).astype(jnp.bfloat16)
    paired = jnp.concatenate([saved_keys, saved_values], axis=1)
    padded = jnp.concatenate([jnp.zeros(((WIN - 1) * BLK, 2 * KVW), jnp.bfloat16), paired], axis=0)
    summary = paired.reshape(N_CTX, BLK, 2 * KVW)[::STRIDE].reshape(SUMMARY * BLK, 2 * KVW)
    keys_total = (WIN + SUMMARY) * BLK

    def one_block(block):
        local = lax.dynamic_slice_in_dim(padded, block * BLK, WIN * BLK, 0)
        kv_all = jnp.concatenate([local, summary], axis=0).astype(jnp.float32)
        key_all = kv_all[:, :KVW].reshape(keys_total, KV_HEADS, HEAD_DIM)
        value_all = kv_all[:, KVW:].reshape(keys_total, KV_HEADS, HEAD_DIM)
        query_blk = lax.dynamic_slice_in_dim(queries, block * BLK, BLK, 0)
        query_blk = query_blk.astype(jnp.float32).reshape(BLK, KV_HEADS, GROUP, HEAD_DIM)
        grad_blk = lax.dynamic_slice_in_dim(grad_out, block * BLK, BLK, 0)
        grad_blk = grad_blk.astype(jnp.float32).reshape(BLK, KV_HEADS, GROUP, HEAD_DIM)
        allowed = block_allowed(block, window, stride, SUMMARY)[:, None]
        scores = jnp.einsum("qhgd,khd->hgqk", query_blk, key_all) * scale
        scores = jnp.where(allowed, scores, jnp.float32(-1e30))
        row_peak = jnp.max(scores, axis=3, keepdims=True)
        weights = jnp.exp(scores - row_peak)
        probs = weights / jnp.sum(weights, axis=3, keepdims=True)
        grad_prob = jnp.einsum("qhgd,khd->hgqk", grad_blk, value_all)
        row_delta = jnp.sum(probs * grad_prob, axis=3, keepdims=True)
        dscore = (probs * (grad_prob - row_delta) * scale).astype(jnp.bfloat16).astype(jnp.float32)
        probs_round = probs.astype(jnp.bfloat16).astype(jnp.float32)
        dquery = jnp.einsum("hgqk,khd->qhgd", dscore, key_all).reshape(BLK, FEAT)
        key_grad = jnp.einsum("hgqk,qhgd->khd", dscore, query_blk).reshape(keys_total, KVW)
        value_grad = jnp.einsum("hgqk,qhgd->khd", probs_round, grad_blk).reshape(keys_total, KVW)
        return dquery, jnp.concatenate([key_grad, value_grad], axis=1)

    dquery_all, parts = lax.map(one_block, jnp.arange(N_CTX, dtype=jnp.int32))
    result = (grad_out.astype(jnp.float32) + gain * dquery_all.reshape(SEQ, FEAT)).astype(jnp.bfloat16)
    local_parts = parts[:, :WIN * BLK].reshape(N_CTX, WIN, BLK, 2 * KVW)
    total = local_parts[:, WIN - 1]
    for offset in range(1, WIN):
        shifted = jnp.concatenate([local_parts[offset:, WIN - 1 - offset], jnp.zeros((offset, BLK, 2 * KVW), jnp.float32)], axis=0)
        total = total + lax.optimization_barrier(shifted.astype(jnp.bfloat16)).astype(jnp.float32)
    strided_sum = jnp.sum(parts[:, WIN * BLK:], axis=0).reshape(SUMMARY, BLK, 2 * KVW)
    total = total.reshape(SUMMARY, STRIDE, BLK, 2 * KVW).at[:, 0].add(strided_sum).reshape(SEQ, 2 * KVW)
    return result, total[:, :KVW].astype(jnp.bfloat16), total[:, KVW:].astype(jnp.bfloat16)


def reference(inputs, saved_keys, saved_values, query_gain, first_grads, head_grads, window, stride):
    grad_table = [[None] * TICKS for layer in range(LAYERS)]
    key_table = [[None] * TICKS for layer in range(LAYERS)]
    value_table = [[None] * TICKS for layer in range(LAYERS)]
    for step_index in range(TICKS):
        for layer in range(LAYERS):
            if step_index == 0:
                grad_out = first_grads[layer]
            elif layer == LAYERS - 1:
                grad_out = head_grads[step_index - 1]
            else:
                grad_out = grad_table[layer + 1][step_index - 1]
            result, key_grad, value_grad = layer_backward(inputs[layer, step_index], saved_keys[layer, step_index], saved_values[layer, step_index], query_gain[layer], grad_out, window[layer], stride[layer])
            grad_table[layer][step_index] = result
            key_table[layer][step_index] = key_grad
            value_table[layer][step_index] = value_grad
    grads_out = jnp.stack([jnp.stack(row, 0) for row in grad_table], 0)
    key_grads = jnp.stack([jnp.stack(row, 0) for row in key_table], 0)
    value_grads = jnp.stack([jnp.stack(row, 0) for row in value_table], 0)
    return grads_out, key_grads, value_grads
```

```python
import functools

import jax
import jax.numpy as jnp
from jax import lax
from jax.experimental import pallas as pl
from jax.experimental.pallas import tpu as pltpu
from jax.sharding import PartitionSpec as P

BLK = 64
WIN = 7
STRIDE = 16
HEAD_DIM = 128
PLANE = 4
SPAN = PLANE * BLK
PREV = (WIN - 1) * BLK
FAR = PREV - SPAN
OWN = PREV
STRIDED = PREV + SPAN
MESH = pl.DeviceIdType.MESH
LOG2E = 1.4426950408889634


def rows_at(start, size):
    return pl.ds(pl.multiple_of(start, BLK), size)


def columns_at(start, size):
    return pl.ds(pl.multiple_of(start, HEAD_DIM), size)


def kernel(
    n_ctx, n_pp, ticks, group,
    inputs, keys, values, gain, first, head, window, stride,
    grads_out, key_out, value_out,
    xq, gr, kv, res, acc, stage, near_in, far_in, strided_in, total,
    local_sem, plane_send, plane_recv, z_send, z_recv, str_send, str_recv,
    pass_send, pass_recv, res_send, res_recv,
    back_send, back_recv, sback_send, sback_recv, out_send, out_recv,
):
    planes = n_ctx // PLANE
    owners = n_ctx // STRIDE
    step = STRIDE // PLANE
    width = group * HEAD_DIM
    ctx = lax.axis_index("ctx")
    pp = lax.axis_index("pp")
    z = ctx // PLANE
    me = lax.rem(ctx, PLANE)
    last = pp == n_pp - 1

    def at(plane, place):
        return (plane * PLANE + place, pp)

    barrier = pltpu.get_barrier_semaphore()
    for k in range(1, PLANE):
        pl.semaphore_signal(barrier, inc=1, device_id=at(z, lax.rem(me + k, PLANE)), device_id_type=MESH)
    for k in range(1, planes):
        pl.semaphore_signal(barrier, inc=1, device_id=at(lax.rem(z + k, planes), me), device_id_type=MESH)

    @pl.when(pp > 0)
    def _():
        pl.semaphore_signal(barrier, inc=1, device_id=(ctx, pp - 1), device_id_type=MESH)

    @pl.when(pp < n_pp - 1)
    def _():
        pl.semaphore_signal(barrier, inc=1, device_id=(ctx, pp + 1), device_id_type=MESH)

    def pieces(t, place, source):
        cols = columns_at(place * HEAD_DIM, HEAD_DIM)
        wide = columns_at(place * width, width)
        rows = rows_at(source * BLK, BLK)
        own_rows = rows_at(OWN + source * BLK, BLK)
        grads = first if t == 0 else head
        return (
            (keys.at[0, t, :, cols], kv.at[t, 0, own_rows, :]),
            (values.at[0, t, :, cols], kv.at[t, 1, own_rows, :]),
            (inputs.at[0, t, :, wide], xq.at[t, rows, :]),
            (grads.at[0, :, wide] if t == 0 else grads.at[t - 1, :, wide], gr.at[t, rows, :]),
        )

    def local(t, kind):
        src, dst = pieces(t, me, me)[kind]
        return pltpu.make_async_copy(src, dst, local_sem.at[t, kind])

    def remote(t, kind, k):
        place = lax.rem(me + k, PLANE)
        src, dst = pieces(t, place, me)[kind]
        return pltpu.make_async_remote_copy(
            src, dst, plane_send.at[t, kind, k], plane_recv.at[t, kind, me],
            device_id=at(z, place), device_id_type=MESH)

    def arriving(t, kind, k):
        source = lax.rem(me + PLANE - k, PLANE)
        src, dst = pieces(t, me, source)[kind]
        return pltpu.make_async_remote_copy(
            src, dst, plane_send.at[t, kind, k], plane_recv.at[t, kind, source],
            device_id=at(z, source), device_id_type=MESH)

    def exchange(t, kinds, act):
        def run():
            for kind in kinds:
                act(t, kind)
        if t > 0 and kinds == (3,):
            pl.when(last)(run)
        else:
            run()

    def start(t, kind):
        for k in range(1, PLANE):
            remote(t, kind, k).start()

    def start_local(t, kind):
        local(t, kind).start()

    def finish_in(t, kind):
        local(t, kind).wait()
        for k in range(1, PLANE):
            arriving(t, kind, k).wait_recv()

    def finish_out(t, kind):
        for k in range(1, PLANE):
            remote(t, kind, k).wait_send()

    for t in range(ticks):
        exchange(t, (0, 1, 2), start_local)
        exchange(t, (3,), start_local)

    zero = functools.partial(jnp.zeros, dtype=jnp.bfloat16)

    @pl.when(z == 0)
    def _():
        for t in range(ticks):
            kv[t, :, FAR:PREV, :] = zero((2, SPAN, HEAD_DIM))

    @pl.when(z <= 1)
    def _():
        for t in range(ticks):
            kv[t, :, 0:FAR, :] = zero((2, FAR, HEAD_DIM))

    for q in range(owners):
        @pl.when(z <= step * q)
        def _():
            at_row = STRIDED + q * BLK
            for t in range(ticks):
                kv[t, :, at_row:at_row + BLK, :] = zero((2, BLK, HEAD_DIM))

    acc[...] = jnp.zeros_like(acc)

    pl.semaphore_wait(
        barrier,
        PLANE - 1 + planes - 1 + jnp.where(pp > 0, 1, 0) + jnp.where(last, 0, 1))

    for t in range(ticks):
        exchange(t, (0, 1), start)
        exchange(t, (2,), start)
        exchange(t, (3,), start)

    def near(t):
        return pltpu.make_async_remote_copy(
            kv.at[t, :, OWN:OWN + SPAN, :], kv.at[t, :, FAR:PREV, :], z_send.at[t, 0], z_recv.at[t, 0],
            device_id=at(z + 1, me), device_id_type=MESH)

    def far(t):
        return pltpu.make_async_remote_copy(
            kv.at[t, :, OWN + SPAN - FAR:OWN + SPAN, :], kv.at[t, :, 0:FAR, :], z_send.at[t, 1], z_recv.at[t, 1],
            device_id=at(z + 2, me), device_id_type=MESH)

    def strided(t, q, plane):
        return pltpu.make_async_remote_copy(
            kv.at[t, :, OWN:OWN + BLK, :], kv.at[t, :, STRIDED + q * BLK:STRIDED + (q + 1) * BLK, :],
            str_send.at[t, plane], str_recv.at[t, q], device_id=at(plane, me), device_id_type=MESH)

    def each_strided(act):
        for q in range(owners):
            @pl.when(z == step * q)
            def _():
                for plane in range(step * q + 1, planes):
                    act(q, plane)

    def send_keys(t):
        exchange(t, (0, 1), finish_in)
        pl.when(z + 1 < planes)(lambda: near(t).start())
        pl.when(z + 2 < planes)(lambda: far(t).start())
        each_strided(lambda q, plane: strided(t, q, plane).start())

    def take_keys(t):
        pl.when(z >= 1)(lambda: near(t).wait_recv())
        pl.when(z >= 2)(lambda: far(t).wait_recv())
        for q in range(owners):
            pl.when(z > step * q)(lambda: strided(t, q, 0).wait_recv())

    def result_out(t, b):
        return pltpu.make_async_remote_copy(
            res.at[t, rows_at(b * BLK, BLK), :], grads_out.at[0, t, :, columns_at(me * width, width)],
            res_send.at[t, b], res_recv.at[t, me], device_id=at(z, b), device_id_type=MESH)

    def result_in(t, source):
        return pltpu.make_async_remote_copy(
            res.at[t, rows_at(me * BLK, BLK), :], grads_out.at[0, t, :, columns_at(source * width, width)],
            res_send.at[t, me], res_recv.at[t, source], device_id=at(z, source), device_id_type=MESH)

    def result_local(t):
        return pltpu.make_async_copy(
            res.at[t, rows_at(me * BLK, BLK), :], grads_out.at[0, t, :, columns_at(me * width, width)],
            local_sem.at[t, 4])

    def relay(t, b):
        rows = rows_at(b * BLK, BLK)
        return pltpu.make_async_remote_copy(
            res.at[t, rows, :], gr.at[t + 1, rows, :], pass_send.at[t, b], pass_recv.at[t, b],
            device_id=(ctx, jnp.maximum(pp - 1, 0)), device_id_type=MESH)

    def near_back(t):
        return pltpu.make_async_remote_copy(
            stage.at[t, :, FAR:PREV, :], near_in.at[t], back_send.at[t, 0], back_recv.at[t, 0],
            device_id=at(z - 1, me), device_id_type=MESH)

    def far_back(t):
        return pltpu.make_async_remote_copy(
            stage.at[t, :, 0:FAR, :], far_in.at[t], back_send.at[t, 1], back_recv.at[t, 1],
            device_id=at(z - 2, me), device_id_type=MESH)

    def strided_back(t, q, plane):
        return pltpu.make_async_remote_copy(
            stage.at[t, :, STRIDED + q * BLK:STRIDED + (q + 1) * BLK, :], strided_in.at[t, plane],
            sback_send.at[t, q], sback_recv.at[t, plane], device_id=at(step * q, me), device_id_type=MESH)

    my_window = window[0, me]
    my_stride = stride[0, me]
    my_gain = gain[0:1, columns_at(me * width, width)]
    key_count = WIN * BLK + owners * BLK
    row_ids = lax.broadcasted_iota(jnp.int32, (BLK, key_count), 0)
    col_ids = lax.broadcasted_iota(jnp.int32, (BLK, key_count), 1)
    col_block = col_ids // BLK
    is_local = col_block < WIN
    key_offset = col_block - (WIN - 1)
    in_window = key_offset > -my_window
    causal = col_ids <= row_ids + (WIN - 1) * BLK
    strided_block = (col_block - WIN) * STRIDE
    scale = HEAD_DIM ** -0.5
    contract = (((1,), (1,)), ((), ()))
    across = (((0,), (0,)), ((), ()))

    def block_step(t, b):
        block = z * PLANE + b
        key_block = jnp.where(is_local, block + key_offset, strided_block)
        on_stride = (key_block & (my_stride - 1)) == 0
        allowed_local = (key_block >= 0) & causal & (in_window | on_stride)
        allowed_far = on_stride & (key_block <= block - WIN)
        allowed = jnp.where(is_local, jnp.where(allowed_local, 1, 0), jnp.where(allowed_far, 1, 0)) == 1
        rows = slice(b * BLK, (b + 1) * BLK)
        local_rows = slice(b * BLK, (b + WIN) * BLK)
        far_rows = slice(STRIDED, STRIDED + owners * BLK)
        key_b = jnp.concatenate([kv[t, 0, local_rows, :], kv[t, 0, far_rows, :]], axis=0)
        value_b = jnp.concatenate([kv[t, 1, local_rows, :], kv[t, 1, far_rows, :]], axis=0)
        queries = (xq[t, rows, :].astype(jnp.float32) * my_gain).astype(jnp.bfloat16)
        grad = gr[t, rows, :]

        def stack(matrix):
            return jnp.concatenate([matrix[:, h * HEAD_DIM:(h + 1) * HEAD_DIM] for h in range(group)], axis=0)

        query_b, grad_b = stack(queries), stack(grad)
        scores = lax.dot_general(query_b, key_b, contract, preferred_element_type=jnp.float32)
        scores = scores.reshape(group, BLK, key_count)
        scores = jnp.where(allowed[None], scores, jnp.float32(-1e30))
        peak = jnp.max(scores, axis=2, keepdims=True)
        weights = jnp.exp2((scores - peak) * jnp.float32(scale * LOG2E))
        probs = weights * (1.0 / jnp.sum(weights, axis=2, keepdims=True))
        grad_prob = lax.dot_general(grad_b, value_b, contract, preferred_element_type=jnp.float32)
        grad_prob = grad_prob.reshape(group, BLK, key_count)
        delta = jnp.sum(probs * grad_prob, axis=2, keepdims=True)
        dscore = (probs * (grad_prob - delta) * jnp.float32(scale)).astype(jnp.bfloat16)
        dscore = dscore.reshape(group * BLK, key_count)
        probs = probs.astype(jnp.bfloat16).reshape(group * BLK, key_count)
        dquery = jnp.dot(dscore, key_b, preferred_element_type=jnp.float32)
        dquery = jnp.concatenate([dquery[h * BLK:(h + 1) * BLK] for h in range(group)], axis=1)
        res[t, rows, :] = (grad.astype(jnp.float32) + my_gain * dquery).astype(jnp.bfloat16)
        for part, term in enumerate((
            lax.dot_general(dscore, query_b, across, preferred_element_type=jnp.float32),
            lax.dot_general(probs, grad_b, across, preferred_element_type=jnp.float32),
        )):
            acc[t, part, local_rows, :] += term[:WIN * BLK]
            acc[t, part, far_rows, :] += term[WIN * BLK:]

    for t in range(ticks):
        send_keys(t)
    for t in range(ticks):
        exchange(t, (2,), finish_in)
        if t == 0:
            finish_in(t, 3)
        else:
            pl.when(last)(lambda: finish_in(t, 3))

            @pl.when(pp < n_pp - 1)
            def _():
                for b in range(PLANE):
                    relay(t - 1, b).wait_recv()
        take_keys(t)
        for b in range(PLANE):
            block_step(t, b)
            if t + 1 < ticks:
                pl.when(pp > 0)(lambda: relay(t, b).start())
            pl.when(me != b)(lambda: result_out(t, b).start())
            if b * BLK + BLK == FAR:
                stage[t, :, 0:FAR, :] = acc[t, :, 0:FAR, :].astype(jnp.bfloat16)
                pl.when(z >= 2)(lambda: far_back(t).start())
        result_local(t).start()
        stage[t, :, FAR:PREV, :] = acc[t, :, FAR:PREV, :].astype(jnp.bfloat16)
        pl.when(z >= 1)(lambda: near_back(t).start())
        stage[t, :, STRIDED:, :] = acc[t, :, STRIDED:, :].astype(jnp.bfloat16)
        for q in range(owners):
            pl.when(z > step * q)(lambda: strided_back(t, q, z).start())

    outs = (key_out, value_out)

    def total_out(t, part, k):
        b = lax.rem(me + k, PLANE)
        return pltpu.make_async_remote_copy(
            total.at[t, part, rows_at(b * BLK, BLK), :],
            outs[part].at[0, t, :, columns_at(me * HEAD_DIM, HEAD_DIM)],
            out_send.at[t, part, k], out_recv.at[t, part, me], device_id=at(z, b), device_id_type=MESH)

    def total_in(t, part, k):
        source = lax.rem(me + PLANE - k, PLANE)
        return pltpu.make_async_remote_copy(
            total.at[t, part, rows_at(me * BLK, BLK), :],
            outs[part].at[0, t, :, columns_at(source * HEAD_DIM, HEAD_DIM)],
            out_send.at[t, part, k], out_recv.at[t, part, source], device_id=at(z, source), device_id_type=MESH)

    def total_local(t, part):
        return pltpu.make_async_copy(
            total.at[t, part, rows_at(me * BLK, BLK), :],
            outs[part].at[0, t, :, columns_at(me * HEAD_DIM, HEAD_DIM)], local_sem.at[t, 5 + part])

    for t in range(ticks):
        @pl.when(z + 1 < planes)
        def _():
            near_back(t).wait_recv()
            acc[t, :, OWN:OWN + SPAN, :] += near_in[t].astype(jnp.float32)

        @pl.when(z + 2 < planes)
        def _():
            far_back(t).wait_recv()
            acc[t, :, OWN + SPAN - FAR:OWN + SPAN, :] += far_in[t].astype(jnp.float32)

        def add_strided(q, plane):
            strided_back(t, q, plane).wait_recv()
            acc[t, :, OWN:OWN + BLK, :] += strided_in[t, plane].astype(jnp.float32)

        each_strided(add_strided)
        total[t] = acc[t, :, OWN:OWN + SPAN, :].astype(jnp.bfloat16)
        for part in range(2):
            for k in range(1, PLANE):
                total_out(t, part, k).start()
            total_local(t, part).start()

    for t in range(ticks):
        exchange(t, (0, 1, 2), finish_out)
        exchange(t, (3,), finish_out)
        pl.when(z + 1 < planes)(lambda: near(t).wait_send())
        pl.when(z + 2 < planes)(lambda: far(t).wait_send())
        each_strided(lambda q, plane: strided(t, q, plane).wait_send())
        for b in range(PLANE):
            if t + 1 < ticks:
                pl.when(pp > 0)(lambda: relay(t, b).wait_send())
            pl.when(me != b)(lambda: result_out(t, b).wait_send())
        pl.when(z >= 2)(lambda: far_back(t).wait_send())
        pl.when(z >= 1)(lambda: near_back(t).wait_send())
        for q in range(owners):
            pl.when(z > step * q)(lambda: strided_back(t, q, z).wait_send())
        result_local(t).wait()
        for k in range(1, PLANE):
            result_in(t, lax.rem(me + k, PLANE)).wait_recv()
        for part in range(2):
            total_local(t, part).wait()
            for k in range(1, PLANE):
                total_out(t, part, k).wait_send()
                total_in(t, part, k).wait_recv()


def body(n_ctx, n_pp, inputs, keys, values, gain, first, head, window, stride):
    ticks = inputs.shape[1]
    feat = inputs.shape[-1]
    kv_heads = keys.shape[-1] // HEAD_DIM
    group = feat // (kv_heads * HEAD_DIM)
    planes = n_ctx // PLANE
    owners = n_ctx // STRIDE
    rows = STRIDED + owners * BLK
    width = group * HEAD_DIM
    bf16, f32 = jnp.bfloat16, jnp.float32
    dma = pltpu.SemaphoreType.DMA
    anywhere = pl.BlockSpec(memory_space=pl.ANY)
    scalars = pl.BlockSpec(memory_space=pltpu.SMEM)
    return pl.pallas_call(
        functools.partial(kernel, n_ctx, n_pp, ticks, group),
        out_shape=[jax.ShapeDtypeStruct(a.shape, bf16) for a in (inputs, keys, values)],
        in_specs=[anywhere] * 3 + [pl.BlockSpec(memory_space=pltpu.VMEM)] + [anywhere] * 2 + [scalars] * 2,
        out_specs=[anywhere] * 3,
        scratch_shapes=[
            pltpu.VMEM((ticks, SPAN, width), bf16),
            pltpu.VMEM((ticks, SPAN, width), bf16),
            pltpu.VMEM((ticks, 2, rows, HEAD_DIM), bf16),
            pltpu.VMEM((ticks, SPAN, width), bf16),
            pltpu.VMEM((ticks, 2, rows, HEAD_DIM), f32),
            pltpu.VMEM((ticks, 2, rows, HEAD_DIM), bf16),
            pltpu.VMEM((ticks, 2, SPAN, HEAD_DIM), bf16),
            pltpu.VMEM((ticks, 2, FAR, HEAD_DIM), bf16),
            pltpu.VMEM((ticks, planes, 2, BLK, HEAD_DIM), bf16),
            pltpu.VMEM((ticks, 2, SPAN, HEAD_DIM), bf16),
            dma((ticks, 7)),
            dma((ticks, 4, PLANE)), dma((ticks, 4, PLANE)),
            dma((ticks, 2)), dma((ticks, 2)),
            dma((ticks, planes)), dma((ticks, owners)),
            dma((ticks, PLANE)), dma((ticks, PLANE)),
            dma((ticks, PLANE)), dma((ticks, PLANE)),
            dma((ticks, 2)), dma((ticks, 2)),
            dma((ticks, owners)), dma((ticks, planes)),
            dma((ticks, 2, PLANE)), dma((ticks, 2, PLANE)),
        ],
        compiler_params=pltpu.CompilerParams(
            collective_id=0, has_side_effects=True, vmem_limit_bytes=40 * 1024 * 1024),
        name="plane_backward",
    )(inputs, keys, values, gain, first, head, window, stride)


def solution(mesh):
    in_specs = (
        P("pp", None, "ctx", None),
        P("pp", None, "ctx", None),
        P("pp", None, "ctx", None),
        P("pp", None),
        P("pp", "ctx", None),
        P(None, "ctx", None),
        P("pp", None),
        P("pp", None),
    )
    out_specs = (P("pp", None, "ctx", None), P("pp", None, "ctx", None), P("pp", None, "ctx", None))
    run = functools.partial(body, mesh.shape["ctx"], mesh.shape["pp"])
    return jax.shard_map(run, mesh=mesh, in_specs=in_specs, out_specs=out_specs, check_vma=False)
```

```python
import functools

import jax
import jax.numpy as jnp
from jax import lax
from jax.experimental import pallas as pl
from jax.experimental.pallas import tpu as pltpu
from jax.sharding import PartitionSpec as P

BLK = 64
WIN = 7
STRIDE = 16
HEAD_DIM = 128
PLANE = 4
SPAN = PLANE * BLK
PREV = (WIN - 1) * BLK
FAR = PREV - SPAN
OWN = PREV
STRIDED = PREV + SPAN
MESH = pl.DeviceIdType.MESH
LOG2E = 1.4426950408889634


def rows_at(start, size):
    return pl.ds(pl.multiple_of(start, BLK), size)


def columns_at(start, size):
    return pl.ds(pl.multiple_of(start, HEAD_DIM), size)


def kernel(
    n_ctx, n_pp, ticks, group,
    inputs, keys, values, gain_hbm, first, head, window_hbm, stride_hbm,
    grads_out, key_out, value_out,
    xq, gr, kv, res, acc, stage, near_in, far_in, strided_in, total, gain, window, stride, small_sem,
    local_sem, plane_send, plane_recv, z_send, z_recv, str_send, str_recv,
    pass_send, pass_recv, res_send, res_recv,
    back_send, back_recv, sback_send, sback_recv, out_send, out_recv,
):
    planes = n_ctx // PLANE
    owners = n_ctx // STRIDE
    step = STRIDE // PLANE
    width = group * HEAD_DIM
    ctx = lax.axis_index("ctx")
    pp = lax.axis_index("pp")
    z = ctx // PLANE
    me = lax.rem(ctx, PLANE)
    last = pp == n_pp - 1

    def at(plane, place):
        return (plane * PLANE + place, pp)

    barrier = pltpu.get_barrier_semaphore()
    for k in range(1, PLANE):
        pl.semaphore_signal(barrier, inc=1, device_id=at(z, lax.rem(me + k, PLANE)), device_id_type=MESH)
    for k in range(1, planes):
        pl.semaphore_signal(barrier, inc=1, device_id=at(lax.rem(z + k, planes), me), device_id_type=MESH)

    @pl.when(pp > 0)
    def _():
        pl.semaphore_signal(barrier, inc=1, device_id=(ctx, pp - 1), device_id_type=MESH)

    @pl.when(pp < n_pp - 1)
    def _():
        pl.semaphore_signal(barrier, inc=1, device_id=(ctx, pp + 1), device_id_type=MESH)

    def pieces(t, place, source):
        cols = columns_at(place * HEAD_DIM, HEAD_DIM)
        wide = columns_at(place * width, width)
        rows = rows_at(source * BLK, BLK)
        own_rows = rows_at(OWN + source * BLK, BLK)
        grads = first if t == 0 else head
        return (
            (keys.at[0, t, :, cols], kv.at[t, 0, own_rows, :]),
            (values.at[0, t, :, cols], kv.at[t, 1, own_rows, :]),
            (inputs.at[0, t, :, wide], xq.at[t, rows, :]),
            (grads.at[0, :, wide] if t == 0 else grads.at[t - 1, :, wide], gr.at[t, rows, :]),
        )

    def local(t, kind):
        src, dst = pieces(t, me, me)[kind]
        return pltpu.make_async_copy(src, dst, local_sem.at[t, kind])

    def remote(t, kind, k):
        place = lax.rem(me + k, PLANE)
        src, dst = pieces(t, place, me)[kind]
        return pltpu.make_async_remote_copy(
            src, dst, plane_send.at[t, kind, k], plane_recv.at[t, kind, me],
            device_id=at(z, place), device_id_type=MESH)

    def arriving(t, kind, k):
        source = lax.rem(me + PLANE - k, PLANE)
        src, dst = pieces(t, me, source)[kind]
        return pltpu.make_async_remote_copy(
            src, dst, plane_send.at[t, kind, k], plane_recv.at[t, kind, source],
            device_id=at(z, source), device_id_type=MESH)

    def exchange(t, kinds, act):
        def run():
            for kind in kinds:
                act(t, kind)
        if t > 0 and kinds == (3,):
            pl.when(last)(run)
        else:
            run()

    def start(t, kind):
        for k in range(1, PLANE):
            remote(t, kind, k).start()

    def start_local(t, kind):
        local(t, kind).start()

    def finish_in(t, kind):
        local(t, kind).wait()
        for k in range(1, PLANE):
            arriving(t, kind, k).wait_recv()

    def finish_out(t, kind):
        for k in range(1, PLANE):
            remote(t, kind, k).wait_send()

    small = [
        pltpu.make_async_copy(src, dst, small_sem.at[i])
        for i, (src, dst) in enumerate(((gain_hbm, gain), (window_hbm, window), (stride_hbm, stride)))
    ]
    for copy in small:
        copy.start()
    for t in range(ticks):
        exchange(t, (0, 1, 2), start_local)
        exchange(t, (3,), start_local)

    zero = functools.partial(jnp.zeros, dtype=jnp.bfloat16)

    @pl.when(z == 0)
    def _():
        for t in range(ticks):
            kv[t, :, FAR:PREV, :] = zero((2, SPAN, HEAD_DIM))

    @pl.when(z <= 1)
    def _():
        for t in range(ticks):
            kv[t, :, 0:FAR, :] = zero((2, FAR, HEAD_DIM))

    for q in range(owners):
        @pl.when(z <= step * q)
        def _():
            at_row = STRIDED + q * BLK
            for t in range(ticks):
                kv[t, :, at_row:at_row + BLK, :] = zero((2, BLK, HEAD_DIM))

    acc[...] = jnp.zeros_like(acc)

    pl.semaphore_wait(
        barrier,
        PLANE - 1 + planes - 1 + jnp.where(pp > 0, 1, 0) + jnp.where(last, 0, 1))

    for t in range(ticks):
        exchange(t, (0, 1), start)
        exchange(t, (2,), start)
        exchange(t, (3,), start)

    def near(t):
        return pltpu.make_async_remote_copy(
            kv.at[t, :, OWN:OWN + SPAN, :], kv.at[t, :, FAR:PREV, :], z_send.at[t, 0], z_recv.at[t, 0],
            device_id=at(z + 1, me), device_id_type=MESH)

    def far(t):
        return pltpu.make_async_remote_copy(
            kv.at[t, :, OWN + SPAN - FAR:OWN + SPAN, :], kv.at[t, :, 0:FAR, :], z_send.at[t, 1], z_recv.at[t, 1],
            device_id=at(z + 2, me), device_id_type=MESH)

    def strided(t, q, plane):
        return pltpu.make_async_remote_copy(
            kv.at[t, :, OWN:OWN + BLK, :], kv.at[t, :, STRIDED + q * BLK:STRIDED + (q + 1) * BLK, :],
            str_send.at[t, plane], str_recv.at[t, q], device_id=at(plane, me), device_id_type=MESH)

    def each_strided(act):
        for q in range(owners):
            @pl.when(z == step * q)
            def _():
                for plane in range(step * q + 1, planes):
                    act(q, plane)

    def send_keys(t):
        exchange(t, (0, 1), finish_in)
        pl.when(z + 1 < planes)(lambda: near(t).start())
        pl.when(z + 2 < planes)(lambda: far(t).start())
        each_strided(lambda q, plane: strided(t, q, plane).start())

    def take_keys(t):
        pl.when(z >= 1)(lambda: near(t).wait_recv())
        pl.when(z >= 2)(lambda: far(t).wait_recv())
        for q in range(owners):
            pl.when(z > step * q)(lambda: strided(t, q, 0).wait_recv())

    def result_out(t, b):
        return pltpu.make_async_remote_copy(
            res.at[t, rows_at(b * BLK, BLK), :], grads_out.at[0, t, :, columns_at(me * width, width)],
            res_send.at[t, b], res_recv.at[t, me], device_id=at(z, b), device_id_type=MESH)

    def result_in(t, source):
        return pltpu.make_async_remote_copy(
            res.at[t, rows_at(me * BLK, BLK), :], grads_out.at[0, t, :, columns_at(source * width, width)],
            res_send.at[t, me], res_recv.at[t, source], device_id=at(z, source), device_id_type=MESH)

    def result_local(t):
        return pltpu.make_async_copy(
            res.at[t, rows_at(me * BLK, BLK), :], grads_out.at[0, t, :, columns_at(me * width, width)],
            local_sem.at[t, 4])

    def relay(t, b):
        rows = rows_at(b * BLK, BLK)
        return pltpu.make_async_remote_copy(
            res.at[t, rows, :], gr.at[t + 1, rows, :], pass_send.at[t, b], pass_recv.at[t, b],
            device_id=(ctx, jnp.maximum(pp - 1, 0)), device_id_type=MESH)

    def near_back(t):
        return pltpu.make_async_remote_copy(
            stage.at[t, :, FAR:PREV, :], near_in.at[t], back_send.at[t, 0], back_recv.at[t, 0],
            device_id=at(z - 1, me), device_id_type=MESH)

    def far_back(t):
        return pltpu.make_async_remote_copy(
            stage.at[t, :, 0:FAR, :], far_in.at[t], back_send.at[t, 1], back_recv.at[t, 1],
            device_id=at(z - 2, me), device_id_type=MESH)

    def strided_back(t, q, plane):
        return pltpu.make_async_remote_copy(
            stage.at[t, :, STRIDED + q * BLK:STRIDED + (q + 1) * BLK, :], strided_in.at[t, plane],
            sback_send.at[t, q], sback_recv.at[t, plane], device_id=at(step * q, me), device_id_type=MESH)

    for copy in small:
        copy.wait()
    my_window = window[0, me]
    my_stride = stride[0, me]
    my_gain = gain[0:1, columns_at(me * width, width)]
    key_ids = lax.broadcasted_iota(jnp.int32, (BLK, group * BLK), 0)
    query_ids = lax.broadcasted_iota(jnp.int32, (BLK, group * BLK), 1) % BLK
    causal = jnp.where(key_ids <= query_ids, jnp.float32(0), jnp.float32(-1e30))
    scale = HEAD_DIM ** -0.5
    contract = (((1,), (1,)), ((), ()))
    rows_of = lambda matrix, c: matrix[c * BLK:(c + 1) * BLK]

    def bias(block, c):
        if c < WIN:
            distance = WIN - 1 - c
            key_block = block - distance
            near_enough = jnp.where(distance < my_window, 1, 0)
            on_stride = jnp.where((key_block & (my_stride - 1)) == 0, 1, 0)
            inside = jnp.where(key_block >= 0, 1, 0)
            allowed = inside * jnp.maximum(near_enough, on_stride)
        else:
            key_block = (c - WIN) * STRIDE
            on_stride = jnp.where((key_block & (my_stride - 1)) == 0, 1, 0)
            allowed = on_stride * jnp.where(key_block <= block - WIN, 1, 0)
        return jnp.where(allowed == 1, jnp.float32(0), jnp.float32(-1e30))

    def block_step(t, b):
        block = z * PLANE + b
        rows = slice(b * BLK, (b + 1) * BLK)
        local_rows = slice(b * BLK, (b + WIN) * BLK)
        far_rows = slice(STRIDED, STRIDED + owners * BLK)
        key_b = jnp.concatenate([kv[t, 0, local_rows, :], kv[t, 0, far_rows, :]], axis=0)
        value_b = jnp.concatenate([kv[t, 1, local_rows, :], kv[t, 1, far_rows, :]], axis=0)
        queries = (xq[t, rows, :].astype(jnp.float32) * my_gain).astype(jnp.bfloat16)
        grad = gr[t, rows, :]

        def stack(matrix):
            return jnp.concatenate([matrix[:, h * HEAD_DIM:(h + 1) * HEAD_DIM] for h in range(group)], axis=0)

        query_b, grad_b = stack(queries), stack(grad)
        scores = lax.dot_general(key_b, query_b, contract, preferred_element_type=jnp.float32)
        scores = jnp.concatenate(
            [rows_of(scores, c) + (causal if c == WIN - 1 else bias(block, c)) for c in range(WIN + owners)], axis=0)
        peak = jnp.max(scores, axis=0, keepdims=True)
        weights = jnp.exp2((scores - peak) * jnp.float32(scale * LOG2E))
        inverse = 1.0 / jnp.sum(weights, axis=0, keepdims=True)
        grad_prob = lax.dot_general(value_b, grad_b, contract, preferred_element_type=jnp.float32)
        probs = weights * inverse
        delta = jnp.sum(probs * grad_prob, axis=0, keepdims=True)
        dscore = (probs * (grad_prob - delta) * jnp.float32(scale)).astype(jnp.bfloat16)
        probs = probs.astype(jnp.bfloat16)
        dquery = jnp.dot(key_b.T, dscore, preferred_element_type=jnp.float32).T
        dquery = jnp.concatenate([rows_of(dquery, h) for h in range(group)], axis=1)
        res[t, rows, :] = (grad.astype(jnp.float32) + my_gain * dquery).astype(jnp.bfloat16)
        for part, term in enumerate((
            jnp.dot(dscore, query_b, preferred_element_type=jnp.float32),
            jnp.dot(probs, grad_b, preferred_element_type=jnp.float32),
        )):
            acc[t, part, local_rows, :] += term[:WIN * BLK]
            acc[t, part, far_rows, :] += term[WIN * BLK:]

    outs = (key_out, value_out)

    def total_out(t, part, k):
        b = lax.rem(me + k, PLANE)
        return pltpu.make_async_remote_copy(
            total.at[t, part, rows_at(b * BLK, BLK), :],
            outs[part].at[0, t, :, columns_at(me * HEAD_DIM, HEAD_DIM)],
            out_send.at[t, part, k], out_recv.at[t, part, me], device_id=at(z, b), device_id_type=MESH)

    def total_in(t, part, k):
        source = lax.rem(me + PLANE - k, PLANE)
        return pltpu.make_async_remote_copy(
            total.at[t, part, rows_at(me * BLK, BLK), :],
            outs[part].at[0, t, :, columns_at(source * HEAD_DIM, HEAD_DIM)],
            out_send.at[t, part, k], out_recv.at[t, part, source], device_id=at(z, source), device_id_type=MESH)

    def total_local(t, part):
        return pltpu.make_async_copy(
            total.at[t, part, rows_at(me * BLK, BLK), :],
            outs[part].at[0, t, :, columns_at(me * HEAD_DIM, HEAD_DIM)], local_sem.at[t, 5 + part])

    def finish(t):
        @pl.when(z + 1 < planes)
        def _():
            near_back(t).wait_recv()
            acc[t, :, OWN:OWN + SPAN, :] += near_in[t].astype(jnp.float32)

        @pl.when(z + 2 < planes)
        def _():
            far_back(t).wait_recv()
            acc[t, :, OWN + SPAN - FAR:OWN + SPAN, :] += far_in[t].astype(jnp.float32)

        def add_strided(q, plane):
            strided_back(t, q, plane).wait_recv()
            acc[t, :, OWN:OWN + BLK, :] += strided_in[t, plane].astype(jnp.float32)

        each_strided(add_strided)
        total[t] = acc[t, :, OWN:OWN + SPAN, :].astype(jnp.bfloat16)
        for part in range(2):
            for k in range(1, PLANE):
                total_out(t, part, k).start()
            total_local(t, part).start()

    send_keys(0)
    for t in range(ticks):
        exchange(t, (2,), finish_in)
        if t == 0:
            finish_in(t, 3)
        else:
            pl.when(last)(lambda: finish_in(t, 3))

            @pl.when(pp < n_pp - 1)
            def _():
                for b in range(PLANE):
                    relay(t - 1, b).wait_recv()
        take_keys(t)
        for b in range(PLANE):
            block_step(t, b)
            if b == 0 and t + 1 < ticks:
                send_keys(t + 1)
            if t + 1 < ticks:
                pl.when(pp > 0)(lambda: relay(t, b).start())
            pl.when(me != b)(lambda: result_out(t, b).start())
            if b * BLK + BLK == FAR:
                stage[t, :, 0:FAR, :] = acc[t, :, 0:FAR, :].astype(jnp.bfloat16)
                pl.when(z >= 2)(lambda: far_back(t).start())
            if t > 0 and b == PLANE - 2:
                finish(t - 1)
        result_local(t).start()
        stage[t, :, FAR:PREV, :] = acc[t, :, FAR:PREV, :].astype(jnp.bfloat16)
        pl.when(z >= 1)(lambda: near_back(t).start())
        stage[t, :, STRIDED:, :] = acc[t, :, STRIDED:, :].astype(jnp.bfloat16)
        for q in range(owners):
            pl.when(z > step * q)(lambda: strided_back(t, q, z).start())

    finish(ticks - 1)

    for t in range(ticks):
        exchange(t, (0, 1, 2), finish_out)
        exchange(t, (3,), finish_out)
        pl.when(z + 1 < planes)(lambda: near(t).wait_send())
        pl.when(z + 2 < planes)(lambda: far(t).wait_send())
        each_strided(lambda q, plane: strided(t, q, plane).wait_send())
        for b in range(PLANE):
            if t + 1 < ticks:
                pl.when(pp > 0)(lambda: relay(t, b).wait_send())
            pl.when(me != b)(lambda: result_out(t, b).wait_send())
        pl.when(z >= 2)(lambda: far_back(t).wait_send())
        pl.when(z >= 1)(lambda: near_back(t).wait_send())
        for q in range(owners):
            pl.when(z > step * q)(lambda: strided_back(t, q, z).wait_send())
        result_local(t).wait()
        for k in range(1, PLANE):
            result_in(t, lax.rem(me + k, PLANE)).wait_recv()
        for part in range(2):
            total_local(t, part).wait()
            for k in range(1, PLANE):
                total_out(t, part, k).wait_send()
                total_in(t, part, k).wait_recv()


def hand_out(a, b, c, a_out, b_out, c_out, sem):
    copies = [
        pltpu.make_async_copy(src, dst, sem.at[i])
        for i, (src, dst) in enumerate(((a, a_out), (b, b_out), (c, c_out)))
    ]
    for copy in copies:
        copy.start()
    for copy in copies:
        copy.wait()


def body(n_ctx, n_pp, inputs, keys, values, gain, first, head, window, stride):
    ticks = inputs.shape[1]
    feat = inputs.shape[-1]
    kv_heads = keys.shape[-1] // HEAD_DIM
    group = feat // (kv_heads * HEAD_DIM)
    planes = n_ctx // PLANE
    owners = n_ctx // STRIDE
    rows = STRIDED + owners * BLK
    width = group * HEAD_DIM
    bf16, f32 = jnp.bfloat16, jnp.float32
    dma = pltpu.SemaphoreType.DMA
    anywhere = pl.BlockSpec(memory_space=pl.ANY)
    outs = pl.pallas_call(
        functools.partial(kernel, n_ctx, n_pp, ticks, group),
        out_shape=[jax.ShapeDtypeStruct(a.shape, bf16) for a in (inputs, keys, values)],
        in_specs=[pl.BlockSpec(memory_space=pltpu.HBM)] * 8,
        out_specs=[anywhere] * 3,
        scratch_shapes=[
            pltpu.VMEM((ticks, SPAN, width), bf16),
            pltpu.VMEM((ticks, SPAN, width), bf16),
            pltpu.VMEM((ticks, 2, rows, HEAD_DIM), bf16),
            pltpu.VMEM((ticks, SPAN, width), bf16),
            pltpu.VMEM((ticks, 2, rows, HEAD_DIM), f32),
            pltpu.VMEM((ticks, 2, rows, HEAD_DIM), bf16),
            pltpu.VMEM((ticks, 2, SPAN, HEAD_DIM), bf16),
            pltpu.VMEM((ticks, 2, FAR, HEAD_DIM), bf16),
            pltpu.VMEM((ticks, planes, 2, BLK, HEAD_DIM), bf16),
            pltpu.VMEM((ticks, 2, SPAN, HEAD_DIM), bf16),
            pltpu.VMEM(gain.shape, f32), pltpu.SMEM(window.shape, jnp.int32), pltpu.SMEM(stride.shape, jnp.int32),
            dma((3,)),
            dma((ticks, 7)),
            dma((ticks, 4, PLANE)), dma((ticks, 4, PLANE)),
            dma((ticks, 2)), dma((ticks, 2)),
            dma((ticks, planes)), dma((ticks, owners)),
            dma((ticks, PLANE)), dma((ticks, PLANE)),
            dma((ticks, PLANE)), dma((ticks, PLANE)),
            dma((ticks, 2)), dma((ticks, 2)),
            dma((ticks, owners)), dma((ticks, planes)),
            dma((ticks, 2, PLANE)), dma((ticks, 2, PLANE)),
        ],
        compiler_params=pltpu.CompilerParams(
            collective_id=0, has_side_effects=True, vmem_limit_bytes=64 * 1024 * 1024),
        name="plane_backward",
    )(inputs, keys, values, gain, first, head, window, stride)
    return pl.pallas_call(
        hand_out,
        out_shape=[jax.ShapeDtypeStruct(a.shape, bf16) for a in (inputs, keys, values)],
        in_specs=[anywhere] * 3,
        out_specs=[pl.BlockSpec(memory_space=pltpu.HBM)] * 3,
        scratch_shapes=[dma((3,))],
        compiler_params=pltpu.CompilerParams(vmem_limit_bytes=64 * 1024 * 1024),
        name="hand_out",
    )(*outs)


def solution(mesh):
    in_specs = (
        P("pp", None, "ctx", None),
        P("pp", None, "ctx", None),
        P("pp", None, "ctx", None),
        P("pp", None),
        P("pp", "ctx", None),
        P(None, "ctx", None),
        P("pp", None),
        P("pp", None),
    )
    out_specs = (P("pp", None, "ctx", None), P("pp", None, "ctx", None), P("pp", None, "ctx", None))
    run = functools.partial(body, mesh.shape["ctx"], mesh.shape["pp"])
    return jax.shard_map(run, mesh=mesh, in_specs=in_specs, out_specs=out_specs, check_vma=False)
```

```python
import functools

import jax
import jax.numpy as jnp
from jax import lax
from jax.experimental import pallas as pl
from jax.experimental.pallas import tpu as pltpu
from jax.sharding import PartitionSpec as P

BLK = 64
WIN = 7
STRIDE = 16
HEAD_DIM = 128
PLANE = 4
SPAN = PLANE * BLK
PREV = (WIN - 1) * BLK
FAR = PREV - SPAN
OWN = PREV
STRIDED = PREV + SPAN
MESH = pl.DeviceIdType.MESH
LOG2E = 1.4426950408889634


def rows_at(start, size):
    return pl.ds(pl.multiple_of(start, BLK), size)


def columns_at(start, size):
    return pl.ds(pl.multiple_of(start, HEAD_DIM), size)


def kernel(
    n_ctx, n_pp, ticks, group,
    inputs, keys, values, gain_hbm, first, head, window_hbm, stride_hbm,
    grads_out, key_out, value_out,
    xq, gr, kv, res, acc, stage, near_in, far_in, strided_in, total, gain, window, stride, small_sem,
    local_sem, plane_send, plane_recv, z_send, z_recv, str_send, str_recv,
    pass_send, pass_recv, res_send, res_recv,
    back_send, back_recv, sback_send, sback_recv, out_send, out_recv,
):
    planes = n_ctx // PLANE
    owners = n_ctx // STRIDE
    step = STRIDE // PLANE
    width = group * HEAD_DIM
    ctx = lax.axis_index("ctx")
    pp = lax.axis_index("pp")
    z = ctx // PLANE
    me = lax.rem(ctx, PLANE)
    last = pp == n_pp - 1

    def at(plane, place):
        return (plane * PLANE + place, pp)

    barrier = pltpu.get_barrier_semaphore()
    for k in range(1, PLANE):
        pl.semaphore_signal(barrier, inc=1, device_id=at(z, lax.rem(me + k, PLANE)), device_id_type=MESH)
    for k in range(1, planes):
        pl.semaphore_signal(barrier, inc=1, device_id=at(lax.rem(z + k, planes), me), device_id_type=MESH)

    @pl.when(pp > 0)
    def _():
        pl.semaphore_signal(barrier, inc=1, device_id=(ctx, pp - 1), device_id_type=MESH)

    @pl.when(pp < n_pp - 1)
    def _():
        pl.semaphore_signal(barrier, inc=1, device_id=(ctx, pp + 1), device_id_type=MESH)

    def pieces(t, place, source):
        cols = columns_at(place * HEAD_DIM, HEAD_DIM)
        wide = columns_at(place * width, width)
        rows = rows_at(source * BLK, BLK)
        own_rows = rows_at(OWN + source * BLK, BLK)
        grads = first if t == 0 else head
        return (
            (keys.at[0, t, :, cols], kv.at[t, 0, own_rows, :]),
            (values.at[0, t, :, cols], kv.at[t, 1, own_rows, :]),
            (inputs.at[0, t, :, wide], xq.at[t, rows, :]),
            (grads.at[0, :, wide] if t == 0 else grads.at[t - 1, :, wide], gr.at[t, rows, :]),
        )

    def local(t, kind):
        src, dst = pieces(t, me, me)[kind]
        return pltpu.make_async_copy(src, dst, local_sem.at[t, kind])

    def remote(t, kind, k):
        place = lax.rem(me + k, PLANE)
        src, dst = pieces(t, place, me)[kind]
        return pltpu.make_async_remote_copy(
            src, dst, plane_send.at[t, kind, k], plane_recv.at[t, kind, me],
            device_id=at(z, place), device_id_type=MESH)

    def arriving(t, kind, k):
        source = lax.rem(me + PLANE - k, PLANE)
        src, dst = pieces(t, me, source)[kind]
        return pltpu.make_async_remote_copy(
            src, dst, plane_send.at[t, kind, k], plane_recv.at[t, kind, source],
            device_id=at(z, source), device_id_type=MESH)

    def exchange(t, kinds, act):
        def run():
            for kind in kinds:
                act(t, kind)
        if t > 0 and kinds == (3,):
            pl.when(last)(run)
        else:
            run()

    def start(t, kind):
        for k in range(1, PLANE):
            remote(t, kind, k).start()

    def start_local(t, kind):
        local(t, kind).start()

    def finish_in(t, kind):
        local(t, kind).wait()
        for k in range(1, PLANE):
            arriving(t, kind, k).wait_recv()

    def take_block(t, kind, b):
        pl.when(me == b)(lambda: local(t, kind).wait())

        @pl.when(me != b)
        def _():
            src, dst = pieces(t, me, b)[kind]
            pltpu.make_async_remote_copy(
                src, dst, plane_send.at[t, kind, 0], plane_recv.at[t, kind, b],
                device_id=at(z, b), device_id_type=MESH).wait_recv()

    def finish_out(t, kind):
        for k in range(1, PLANE):
            remote(t, kind, k).wait_send()

    small = [
        pltpu.make_async_copy(src, dst, small_sem.at[i])
        for i, (src, dst) in enumerate(((gain_hbm, gain), (window_hbm, window), (stride_hbm, stride)))
    ]
    for copy in small:
        copy.start()
    for t in range(ticks):
        exchange(t, (0, 1, 2), start_local)
        exchange(t, (3,), start_local)

    zero = functools.partial(jnp.zeros, dtype=jnp.bfloat16)

    @pl.when(z == 0)
    def _():
        for t in range(ticks):
            kv[t, :, FAR:PREV, :] = zero((2, SPAN, HEAD_DIM))

    @pl.when(z <= 1)
    def _():
        for t in range(ticks):
            kv[t, :, 0:FAR, :] = zero((2, FAR, HEAD_DIM))

    for q in range(owners):
        @pl.when(z <= step * q)
        def _():
            at_row = STRIDED + q * BLK
            for t in range(ticks):
                kv[t, :, at_row:at_row + BLK, :] = zero((2, BLK, HEAD_DIM))

    acc[...] = jnp.zeros_like(acc)

    pl.semaphore_wait(
        barrier,
        PLANE - 1 + planes - 1 + jnp.where(pp > 0, 1, 0) + jnp.where(last, 0, 1))

    for t in range(ticks):
        exchange(t, (0, 1), start)
    exchange(0, (2,), start)

    def near(t):
        return pltpu.make_async_remote_copy(
            kv.at[t, :, OWN:OWN + SPAN, :], kv.at[t, :, FAR:PREV, :], z_send.at[t, 0], z_recv.at[t, 0],
            device_id=at(z + 1, me), device_id_type=MESH)

    def far(t):
        return pltpu.make_async_remote_copy(
            kv.at[t, :, OWN + SPAN - FAR:OWN + SPAN, :], kv.at[t, :, 0:FAR, :], z_send.at[t, 1], z_recv.at[t, 1],
            device_id=at(z + 2, me), device_id_type=MESH)

    def strided(t, q, plane):
        return pltpu.make_async_remote_copy(
            kv.at[t, :, OWN:OWN + BLK, :], kv.at[t, :, STRIDED + q * BLK:STRIDED + (q + 1) * BLK, :],
            str_send.at[t, plane], str_recv.at[t, q], device_id=at(plane, me), device_id_type=MESH)

    def each_strided(act):
        for q in range(owners):
            @pl.when(z == step * q)
            def _():
                for plane in range(step * q + 1, planes):
                    act(q, plane)

    def send_keys(t):
        exchange(t, (0, 1), finish_in)
        pl.when(z + 1 < planes)(lambda: near(t).start())
        pl.when(z + 2 < planes)(lambda: far(t).start())
        each_strided(lambda q, plane: strided(t, q, plane).start())

    def take_keys(t):
        pl.when(z >= 1)(lambda: near(t).wait_recv())
        pl.when(z >= 2)(lambda: far(t).wait_recv())
        for q in range(owners):
            pl.when(z > step * q)(lambda: strided(t, q, 0).wait_recv())

    def result_out(t, b):
        return pltpu.make_async_remote_copy(
            res.at[t, rows_at(b * BLK, BLK), :], grads_out.at[0, t, :, columns_at(me * width, width)],
            res_send.at[t, b], res_recv.at[t, me], device_id=at(z, b), device_id_type=MESH)

    def result_in(t, source):
        return pltpu.make_async_remote_copy(
            res.at[t, rows_at(me * BLK, BLK), :], grads_out.at[0, t, :, columns_at(source * width, width)],
            res_send.at[t, me], res_recv.at[t, source], device_id=at(z, source), device_id_type=MESH)

    def result_local(t):
        return pltpu.make_async_copy(
            res.at[t, rows_at(me * BLK, BLK), :], grads_out.at[0, t, :, columns_at(me * width, width)],
            local_sem.at[t, 4])

    def relay(t, b):
        rows = rows_at(b * BLK, BLK)
        return pltpu.make_async_remote_copy(
            res.at[t, rows, :], gr.at[t + 1, rows, :], pass_send.at[t, b], pass_recv.at[t, b],
            device_id=(ctx, jnp.maximum(pp - 1, 0)), device_id_type=MESH)

    def near_back(t):
        return pltpu.make_async_remote_copy(
            stage.at[t, :, FAR:PREV, :], near_in.at[t], back_send.at[t, 0], back_recv.at[t, 0],
            device_id=at(z - 1, me), device_id_type=MESH)

    def far_back(t):
        return pltpu.make_async_remote_copy(
            stage.at[t, :, 0:FAR, :], far_in.at[t], back_send.at[t, 1], back_recv.at[t, 1],
            device_id=at(z - 2, me), device_id_type=MESH)

    def strided_back(t, q, plane):
        return pltpu.make_async_remote_copy(
            stage.at[t, :, STRIDED + q * BLK:STRIDED + (q + 1) * BLK, :], strided_in.at[t, plane],
            sback_send.at[t, q], sback_recv.at[t, plane], device_id=at(step * q, me), device_id_type=MESH)

    for copy in small:
        copy.wait()
    my_window = window[0, me]
    my_stride = stride[0, me]
    my_gain = gain[0:1, columns_at(me * width, width)]
    key_ids = lax.broadcasted_iota(jnp.int32, (BLK, group * BLK), 0)
    query_ids = lax.broadcasted_iota(jnp.int32, (BLK, group * BLK), 1) % BLK
    causal = jnp.where(key_ids <= query_ids, jnp.float32(0), jnp.float32(-1e30))
    scale = HEAD_DIM ** -0.5
    contract = (((1,), (1,)), ((), ()))
    rows_of = lambda matrix, c: matrix[c * BLK:(c + 1) * BLK]

    def bias(block, c):
        if c < WIN:
            distance = WIN - 1 - c
            key_block = block - distance
            near_enough = jnp.where(distance < my_window, 1, 0)
            on_stride = jnp.where((key_block & (my_stride - 1)) == 0, 1, 0)
            inside = jnp.where(key_block >= 0, 1, 0)
            allowed = inside * jnp.maximum(near_enough, on_stride)
        else:
            key_block = (c - WIN) * STRIDE
            on_stride = jnp.where((key_block & (my_stride - 1)) == 0, 1, 0)
            allowed = on_stride * jnp.where(key_block <= block - WIN, 1, 0)
        return jnp.where(allowed == 1, jnp.float32(0), jnp.float32(-1e30))

    def block_step(t, b):
        block = z * PLANE + b
        rows = slice(b * BLK, (b + 1) * BLK)
        local_rows = slice(b * BLK, (b + WIN) * BLK)
        far_rows = slice(STRIDED, STRIDED + owners * BLK)
        key_b = jnp.concatenate([kv[t, 0, local_rows, :], kv[t, 0, far_rows, :]], axis=0)
        value_b = jnp.concatenate([kv[t, 1, local_rows, :], kv[t, 1, far_rows, :]], axis=0)
        queries = (xq[t, rows, :].astype(jnp.float32) * my_gain).astype(jnp.bfloat16)
        grad = gr[t, rows, :]

        def stack(matrix):
            return jnp.concatenate([matrix[:, h * HEAD_DIM:(h + 1) * HEAD_DIM] for h in range(group)], axis=0)

        query_b, grad_b = stack(queries), stack(grad)
        scores = lax.dot_general(key_b, query_b, contract, preferred_element_type=jnp.float32)
        scores = jnp.concatenate(
            [rows_of(scores, c) + (causal if c == WIN - 1 else bias(block, c)) for c in range(WIN + owners)], axis=0)
        peak = jnp.max(scores, axis=0, keepdims=True)
        weights = jnp.exp2((scores - peak) * jnp.float32(scale * LOG2E))
        inverse = 1.0 / jnp.sum(weights, axis=0, keepdims=True)
        grad_prob = lax.dot_general(value_b, grad_b, contract, preferred_element_type=jnp.float32)
        probs = weights * inverse
        delta = jnp.sum(probs * grad_prob, axis=0, keepdims=True)
        dscore = (probs * (grad_prob - delta) * jnp.float32(scale)).astype(jnp.bfloat16)
        probs = probs.astype(jnp.bfloat16)
        dquery = jnp.dot(key_b.T, dscore, preferred_element_type=jnp.float32).T
        dquery = jnp.concatenate([rows_of(dquery, h) for h in range(group)], axis=1)
        res[t, rows, :] = (grad.astype(jnp.float32) + my_gain * dquery).astype(jnp.bfloat16)
        for part, term in enumerate((
            jnp.dot(dscore, query_b, preferred_element_type=jnp.float32),
            jnp.dot(probs, grad_b, preferred_element_type=jnp.float32),
        )):
            acc[t, part, local_rows, :] += term[:WIN * BLK]
            acc[t, part, far_rows, :] += term[WIN * BLK:]

    outs = (key_out, value_out)

    def total_out(t, part, k):
        b = lax.rem(me + k, PLANE)
        return pltpu.make_async_remote_copy(
            total.at[t, part, rows_at(b * BLK, BLK), :],
            outs[part].at[0, t, :, columns_at(me * HEAD_DIM, HEAD_DIM)],
            out_send.at[t, part, k], out_recv.at[t, part, me], device_id=at(z, b), device_id_type=MESH)

    def total_in(t, part, k):
        source = lax.rem(me + PLANE - k, PLANE)
        return pltpu.make_async_remote_copy(
            total.at[t, part, rows_at(me * BLK, BLK), :],
            outs[part].at[0, t, :, columns_at(source * HEAD_DIM, HEAD_DIM)],
            out_send.at[t, part, k], out_recv.at[t, part, source], device_id=at(z, source), device_id_type=MESH)

    def total_local(t, part):
        return pltpu.make_async_copy(
            total.at[t, part, rows_at(me * BLK, BLK), :],
            outs[part].at[0, t, :, columns_at(me * HEAD_DIM, HEAD_DIM)], local_sem.at[t, 5 + part])

    def finish(t):
        @pl.when(z + 1 < planes)
        def _():
            near_back(t).wait_recv()
            acc[t, :, OWN:OWN + SPAN, :] += near_in[t].astype(jnp.float32)

        @pl.when(z + 2 < planes)
        def _():
            far_back(t).wait_recv()
            acc[t, :, OWN + SPAN - FAR:OWN + SPAN, :] += far_in[t].astype(jnp.float32)

        def add_strided(q, plane):
            strided_back(t, q, plane).wait_recv()
            acc[t, :, OWN:OWN + BLK, :] += strided_in[t, plane].astype(jnp.float32)

        each_strided(add_strided)
        total[t] = acc[t, :, OWN:OWN + SPAN, :].astype(jnp.bfloat16)
        for part in range(2):
            for k in range(1, PLANE):
                total_out(t, part, k).start()
            total_local(t, part).start()

    for t in range(ticks):
        send_keys(t)
        if t > 0:
            exchange(t, (2,), start)
        exchange(t, (3,), start)
    for t in range(ticks):
        take_keys(t)
        for b in range(PLANE):
            take_block(t, 2, b)
            if t == 0:
                take_block(t, 3, b)
            else:
                pl.when(last)(lambda: take_block(t, 3, b))
                pl.when(pp < n_pp - 1)(lambda: relay(t - 1, b).wait_recv())
            block_step(t, b)
            if t + 1 < ticks:
                pl.when(pp > 0)(lambda: relay(t, b).start())
            else:
                pl.when(me != b)(lambda: result_out(t, b).start())
            if b * BLK + BLK == FAR:
                stage[t, :, 0:FAR, :] = acc[t, :, 0:FAR, :].astype(jnp.bfloat16)
                pl.when(z >= 2)(lambda: far_back(t).start())
            if t > 0 and b == PLANE - 2:
                finish(t - 1)
        if t + 1 < ticks:
            for b in range(PLANE):
                pl.when(me != b)(lambda: result_out(t, b).start())
        result_local(t).start()
        stage[t, :, FAR:PREV, :] = acc[t, :, FAR:PREV, :].astype(jnp.bfloat16)
        pl.when(z >= 1)(lambda: near_back(t).start())
        stage[t, :, STRIDED:, :] = acc[t, :, STRIDED:, :].astype(jnp.bfloat16)
        for q in range(owners):
            pl.when(z > step * q)(lambda: strided_back(t, q, z).start())

    finish(ticks - 1)

    for t in range(ticks):
        exchange(t, (0, 1, 2), finish_out)
        exchange(t, (3,), finish_out)
        pl.when(z + 1 < planes)(lambda: near(t).wait_send())
        pl.when(z + 2 < planes)(lambda: far(t).wait_send())
        each_strided(lambda q, plane: strided(t, q, plane).wait_send())
        for b in range(PLANE):
            if t + 1 < ticks:
                pl.when(pp > 0)(lambda: relay(t, b).wait_send())
            pl.when(me != b)(lambda: result_out(t, b).wait_send())
        pl.when(z >= 2)(lambda: far_back(t).wait_send())
        pl.when(z >= 1)(lambda: near_back(t).wait_send())
        for q in range(owners):
            pl.when(z > step * q)(lambda: strided_back(t, q, z).wait_send())
        result_local(t).wait()
        for k in range(1, PLANE):
            result_in(t, lax.rem(me + k, PLANE)).wait_recv()
        for part in range(2):
            total_local(t, part).wait()
            for k in range(1, PLANE):
                total_out(t, part, k).wait_send()
                total_in(t, part, k).wait_recv()


def hand_out(a, b, c, a_out, b_out, c_out, sem):
    copies = [
        pltpu.make_async_copy(src, dst, sem.at[i])
        for i, (src, dst) in enumerate(((a, a_out), (b, b_out), (c, c_out)))
    ]
    for copy in copies:
        copy.start()
    for copy in copies:
        copy.wait()


def body(n_ctx, n_pp, inputs, keys, values, gain, first, head, window, stride):
    ticks = inputs.shape[1]
    feat = inputs.shape[-1]
    kv_heads = keys.shape[-1] // HEAD_DIM
    group = feat // (kv_heads * HEAD_DIM)
    planes = n_ctx // PLANE
    owners = n_ctx // STRIDE
    rows = STRIDED + owners * BLK
    width = group * HEAD_DIM
    bf16, f32 = jnp.bfloat16, jnp.float32
    dma = pltpu.SemaphoreType.DMA
    anywhere = pl.BlockSpec(memory_space=pl.ANY)
    outs = pl.pallas_call(
        functools.partial(kernel, n_ctx, n_pp, ticks, group),
        out_shape=[jax.ShapeDtypeStruct(a.shape, bf16) for a in (inputs, keys, values)],
        in_specs=[pl.BlockSpec(memory_space=pltpu.HBM)] * 8,
        out_specs=[anywhere] * 3,
        scratch_shapes=[
            pltpu.VMEM((ticks, SPAN, width), bf16),
            pltpu.VMEM((ticks, SPAN, width), bf16),
            pltpu.VMEM((ticks, 2, rows, HEAD_DIM), bf16),
            pltpu.VMEM((ticks, SPAN, width), bf16),
            pltpu.VMEM((ticks, 2, rows, HEAD_DIM), f32),
            pltpu.VMEM((ticks, 2, rows, HEAD_DIM), bf16),
            pltpu.VMEM((ticks, 2, SPAN, HEAD_DIM), bf16),
            pltpu.VMEM((ticks, 2, FAR, HEAD_DIM), bf16),
            pltpu.VMEM((ticks, planes, 2, BLK, HEAD_DIM), bf16),
            pltpu.VMEM((ticks, 2, SPAN, HEAD_DIM), bf16),
            pltpu.VMEM(gain.shape, f32), pltpu.SMEM(window.shape, jnp.int32), pltpu.SMEM(stride.shape, jnp.int32),
            dma((3,)),
            dma((ticks, 7)),
            dma((ticks, 4, PLANE)), dma((ticks, 4, PLANE)),
            dma((ticks, 2)), dma((ticks, 2)),
            dma((ticks, planes)), dma((ticks, owners)),
            dma((ticks, PLANE)), dma((ticks, PLANE)),
            dma((ticks, PLANE)), dma((ticks, PLANE)),
            dma((ticks, 2)), dma((ticks, 2)),
            dma((ticks, owners)), dma((ticks, planes)),
            dma((ticks, 2, PLANE)), dma((ticks, 2, PLANE)),
        ],
        compiler_params=pltpu.CompilerParams(
            collective_id=0, has_side_effects=True, vmem_limit_bytes=40 * 1024 * 1024),
        name="plane_backward",
    )(*[pltpu.with_memory_space_constraint(a, pltpu.HBM) for a in (inputs, keys, values, gain, first, head, window, stride)])
    return pl.pallas_call(
        hand_out,
        out_shape=[jax.ShapeDtypeStruct(a.shape, bf16) for a in (inputs, keys, values)],
        in_specs=[anywhere] * 3,
        out_specs=[pl.BlockSpec(memory_space=pltpu.HBM)] * 3,
        scratch_shapes=[dma((3,))],
        compiler_params=pltpu.CompilerParams(vmem_limit_bytes=40 * 1024 * 1024),
        name="hand_out",
    )(*outs)


def solution(mesh):
    in_specs = (
        P("pp", None, "ctx", None),
        P("pp", None, "ctx", None),
        P("pp", None, "ctx", None),
        P("pp", None),
        P("pp", "ctx", None),
        P(None, "ctx", None),
        P("pp", None),
        P("pp", None),
    )
    out_specs = (P("pp", None, "ctx", None), P("pp", None, "ctx", None), P("pp", None, "ctx", None))
    run = functools.partial(body, mesh.shape["ctx"], mesh.shape["pp"])
    return jax.shard_map(run, mesh=mesh, in_specs=in_specs, out_specs=out_specs, check_vma=False)
```

```python
import functools

import jax
import jax.numpy as jnp
from jax import lax
from jax.experimental import pallas as pl
from jax.experimental.pallas import tpu as pltpu
from jax.sharding import PartitionSpec as P

BLK = 64
WIN = 7
STRIDE = 16
HEAD_DIM = 128
PLANE = 4
SPAN = PLANE * BLK
PREV = (WIN - 1) * BLK
FAR = PREV - SPAN
OWN = PREV
PAIR_KEYS = WIN + 1
STRIDED = PREV + SPAN
MESH = pl.DeviceIdType.MESH
LOG2E = 1.4426950408889634


def rows_at(start, size):
    return pl.ds(pl.multiple_of(start, BLK), size)


def columns_at(start, size):
    return pl.ds(pl.multiple_of(start, HEAD_DIM), size)


def kernel(
    n_ctx, n_pp, ticks, group,
    inputs, keys, values, gain_hbm, first, head, window_hbm, stride_hbm,
    grads_out, key_out, value_out,
    xq, gr, kv, res, acc, stage, near_in, far_in, strided_in, total, gain, window, stride, small_sem,
    scores_at, grad_prob_at, probs_at, dscore_at,
    local_sem, plane_send, plane_recv, z_send, z_recv, str_send, str_recv,
    pass_send, pass_recv, res_send, res_recv,
    back_send, back_recv, sback_send, sback_recv, out_send, out_recv,
):
    planes = n_ctx // PLANE
    owners = n_ctx // STRIDE
    step = STRIDE // PLANE
    width = group * HEAD_DIM
    ctx = lax.axis_index("ctx")
    pp = lax.axis_index("pp")
    z = ctx // PLANE
    me = lax.rem(ctx, PLANE)
    last = pp == n_pp - 1

    def at(plane, place):
        return (plane * PLANE + place, pp)

    barrier = pltpu.get_barrier_semaphore()
    for k in range(1, PLANE):
        pl.semaphore_signal(barrier, inc=1, device_id=at(z, lax.rem(me + k, PLANE)), device_id_type=MESH)
    for k in range(1, planes):
        pl.semaphore_signal(barrier, inc=1, device_id=at(lax.rem(z + k, planes), me), device_id_type=MESH)

    @pl.when(pp > 0)
    def _():
        pl.semaphore_signal(barrier, inc=1, device_id=(ctx, pp - 1), device_id_type=MESH)

    @pl.when(pp < n_pp - 1)
    def _():
        pl.semaphore_signal(barrier, inc=1, device_id=(ctx, pp + 1), device_id_type=MESH)

    def pieces(t, place, source):
        cols = columns_at(place * HEAD_DIM, HEAD_DIM)
        wide = columns_at(place * width, width)
        rows = rows_at(source * BLK, BLK)
        own_rows = rows_at(OWN + source * BLK, BLK)
        grads = first if t == 0 else head
        return (
            (keys.at[0, t, :, cols], kv.at[t, 0, own_rows, :]),
            (values.at[0, t, :, cols], kv.at[t, 1, own_rows, :]),
            (inputs.at[0, t, :, wide], xq.at[t, rows, :]),
            (grads.at[0, :, wide] if t == 0 else grads.at[t - 1, :, wide], gr.at[t, rows, :]),
        )

    def local(t, kind):
        src, dst = pieces(t, me, me)[kind]
        return pltpu.make_async_copy(src, dst, local_sem.at[t, kind])

    def remote(t, kind, k):
        place = lax.rem(me + k, PLANE)
        src, dst = pieces(t, place, me)[kind]
        return pltpu.make_async_remote_copy(
            src, dst, plane_send.at[t, kind, k], plane_recv.at[t, kind, me],
            device_id=at(z, place), device_id_type=MESH)

    def arriving(t, kind, k):
        source = lax.rem(me + PLANE - k, PLANE)
        src, dst = pieces(t, me, source)[kind]
        return pltpu.make_async_remote_copy(
            src, dst, plane_send.at[t, kind, k], plane_recv.at[t, kind, source],
            device_id=at(z, source), device_id_type=MESH)

    def exchange(t, kinds, act):
        def run():
            for kind in kinds:
                act(t, kind)
        if t > 0 and kinds == (3,):
            pl.when(last)(run)
        else:
            run()

    def start(t, kind):
        for k in range(1, PLANE):
            remote(t, kind, k).start()

    def start_local(t, kind):
        local(t, kind).start()

    def finish_in(t, kind):
        local(t, kind).wait()
        for k in range(1, PLANE):
            arriving(t, kind, k).wait_recv()

    def take_block(t, kind, b):
        pl.when(me == b)(lambda: local(t, kind).wait())

        @pl.when(me != b)
        def _():
            src, dst = pieces(t, me, b)[kind]
            pltpu.make_async_remote_copy(
                src, dst, plane_send.at[t, kind, 0], plane_recv.at[t, kind, b],
                device_id=at(z, b), device_id_type=MESH).wait_recv()

    def finish_out(t, kind):
        for k in range(1, PLANE):
            remote(t, kind, k).wait_send()

    small = [
        pltpu.make_async_copy(src, dst, small_sem.at[i])
        for i, (src, dst) in enumerate(((gain_hbm, gain), (window_hbm, window), (stride_hbm, stride)))
    ]
    for copy in small:
        copy.start()
    for t in range(ticks):
        exchange(t, (0, 1, 2), start_local)
        exchange(t, (3,), start_local)

    zero = functools.partial(jnp.zeros, dtype=jnp.bfloat16)

    @pl.when(z == 0)
    def _():
        for t in range(ticks):
            kv[t, :, FAR:PREV, :] = zero((2, SPAN, HEAD_DIM))

    @pl.when(z <= 1)
    def _():
        for t in range(ticks):
            kv[t, :, 0:FAR, :] = zero((2, FAR, HEAD_DIM))

    for q in range(owners):
        @pl.when(z <= step * q)
        def _():
            at_row = STRIDED + q * BLK
            for t in range(ticks):
                kv[t, :, at_row:at_row + BLK, :] = zero((2, BLK, HEAD_DIM))

    probs_at[...] = jnp.zeros_like(probs_at)
    dscore_at[...] = jnp.zeros_like(dscore_at)

    pl.semaphore_wait(
        barrier,
        PLANE - 1 + planes - 1 + jnp.where(pp > 0, 1, 0) + jnp.where(last, 0, 1))

    for t in range(ticks):
        exchange(t, (0, 1), start)
        exchange(t, (2,), start)
        exchange(t, (3,), start)

    def near(t):
        return pltpu.make_async_remote_copy(
            kv.at[t, :, OWN:OWN + SPAN, :], kv.at[t, :, FAR:PREV, :], z_send.at[t, 0], z_recv.at[t, 0],
            device_id=at(z + 1, me), device_id_type=MESH)

    def far(t):
        return pltpu.make_async_remote_copy(
            kv.at[t, :, OWN + SPAN - FAR:OWN + SPAN, :], kv.at[t, :, 0:FAR, :], z_send.at[t, 1], z_recv.at[t, 1],
            device_id=at(z + 2, me), device_id_type=MESH)

    def strided(t, q, plane):
        return pltpu.make_async_remote_copy(
            kv.at[t, :, OWN:OWN + BLK, :], kv.at[t, :, STRIDED + q * BLK:STRIDED + (q + 1) * BLK, :],
            str_send.at[t, plane], str_recv.at[t, q], device_id=at(plane, me), device_id_type=MESH)

    def each_strided(act):
        for q in range(owners):
            @pl.when(z == step * q)
            def _():
                for plane in range(step * q + 1, planes):
                    act(q, plane)

    def send_keys(t):
        exchange(t, (0, 1), finish_in)
        pl.when(z + 1 < planes)(lambda: near(t).start())
        pl.when(z + 2 < planes)(lambda: far(t).start())
        each_strided(lambda q, plane: strided(t, q, plane).start())

    def take_keys(t):
        pl.when(z >= 1)(lambda: near(t).wait_recv())
        pl.when(z >= 2)(lambda: far(t).wait_recv())
        for q in range(owners):
            pl.when(z > step * q)(lambda: strided(t, q, 0).wait_recv())

    def result_out(t, b):
        return pltpu.make_async_remote_copy(
            res.at[t, rows_at(b * BLK, BLK), :], grads_out.at[0, t, :, columns_at(me * width, width)],
            res_send.at[t, b], res_recv.at[t, me], device_id=at(z, b), device_id_type=MESH)

    def result_in(t, source):
        return pltpu.make_async_remote_copy(
            res.at[t, rows_at(me * BLK, BLK), :], grads_out.at[0, t, :, columns_at(source * width, width)],
            res_send.at[t, me], res_recv.at[t, source], device_id=at(z, source), device_id_type=MESH)

    def result_local(t):
        return pltpu.make_async_copy(
            res.at[t, rows_at(me * BLK, BLK), :], grads_out.at[0, t, :, columns_at(me * width, width)],
            local_sem.at[t, 4])

    def relay(t, b):
        rows = rows_at(b * BLK, BLK)
        return pltpu.make_async_remote_copy(
            res.at[t, rows, :], gr.at[t + 1, rows, :], pass_send.at[t, b], pass_recv.at[t, b],
            device_id=(ctx, jnp.maximum(pp - 1, 0)), device_id_type=MESH)

    def near_back(t):
        return pltpu.make_async_remote_copy(
            stage.at[t, :, FAR:PREV, :], near_in.at[t], back_send.at[t, 0], back_recv.at[t, 0],
            device_id=at(z - 1, me), device_id_type=MESH)

    def far_back(t):
        return pltpu.make_async_remote_copy(
            stage.at[t, :, 0:FAR, :], far_in.at[t], back_send.at[t, 1], back_recv.at[t, 1],
            device_id=at(z - 2, me), device_id_type=MESH)

    def strided_back(t, q, plane):
        return pltpu.make_async_remote_copy(
            stage.at[t, :, STRIDED + q * BLK:STRIDED + (q + 1) * BLK, :], strided_in.at[t, plane],
            sback_send.at[t, q], sback_recv.at[t, plane], device_id=at(step * q, me), device_id_type=MESH)

    for copy in small:
        copy.wait()
    my_window = window[0, me]
    my_stride = stride[0, me]
    my_gain = gain[0:1, columns_at(me * width, width)]
    key_ids = lax.broadcasted_iota(jnp.int32, (BLK, group * BLK), 0)
    query_ids = lax.broadcasted_iota(jnp.int32, (BLK, group * BLK), 1) % BLK
    causal = jnp.where(key_ids <= query_ids, jnp.float32(0), jnp.float32(-1e30))
    scale = HEAD_DIM ** -0.5
    contract = (((1,), (1,)), ((), ()))
    rows_of = lambda matrix, c: matrix[c * BLK:(c + 1) * BLK]

    def bias(block, c):
        if c < WIN:
            distance = WIN - 1 - c
            key_block = block - distance
            near_enough = jnp.where(distance < my_window, 1, 0)
            on_stride = jnp.where((key_block & (my_stride - 1)) == 0, 1, 0)
            inside = jnp.where(key_block >= 0, 1, 0)
            allowed = inside * jnp.maximum(near_enough, on_stride)
        else:
            key_block = (c - WIN) * STRIDE
            on_stride = jnp.where((key_block & (my_stride - 1)) == 0, 1, 0)
            allowed = on_stride * jnp.where(key_block <= block - WIN, 1, 0)
        return jnp.where(allowed == 1, jnp.float32(0), jnp.float32(-1e30))

    def stack(matrix):
        return jnp.concatenate([matrix[:, h * HEAD_DIM:(h + 1) * HEAD_DIM] for h in range(group)], axis=0)

    def folded(chunk, combine):
        return combine(chunk.reshape(BLK // 8, 8, lanes), axis=0)

    lanes = group * BLK
    factor = jnp.float32(scale * LOG2E)

    def pair_step(t, pair):
        first_row = pair * 2 * BLK
        local_rows = slice(first_row, first_row + PAIR_KEYS * BLK)
        far_rows = slice(STRIDED, STRIDED + owners * BLK)
        key_p = jnp.concatenate([kv[t, 0, local_rows, :], kv[t, 0, far_rows, :]], axis=0)
        value_p = jnp.concatenate([kv[t, 1, local_rows, :], kv[t, 1, far_rows, :]], axis=0)
        rows = slice(first_row, first_row + 2 * BLK)
        queries = (xq[t, rows, :].astype(jnp.float32) * my_gain).astype(jnp.bfloat16)
        grad = gr[t, rows, :]
        query_p = jnp.concatenate([stack(queries[:BLK]), stack(queries[BLK:])], axis=0)
        grad_p = jnp.concatenate([stack(grad[:BLK]), stack(grad[BLK:])], axis=0)
        scores_at[...] = lax.dot_general(key_p, query_p, contract, preferred_element_type=jnp.float32)
        grad_prob_at[...] = lax.dot_general(value_p, grad_p, contract, preferred_element_type=jnp.float32)
        for half in range(2):
            block = z * PLANE + pair * 2 + half
            cols = slice(half * lanes, (half + 1) * lanes)
            chunks = [(c, c - half) for c in range(PAIR_KEYS) if 0 <= c - half < WIN]
            chunks += [(PAIR_KEYS + q, WIN + q) for q in range(owners)]
            biases = [None if kind == WIN - 1 else bias(block, kind) for c, kind in chunks]

            def raw(c, kind):
                chunk = scores_at[c * BLK:(c + 1) * BLK, cols]
                return chunk + causal if kind == WIN - 1 else chunk

            peak = None
            for (c, kind), shift in zip(chunks, biases):
                high = folded(raw(c, kind), jnp.max)
                high = high if shift is None else high + shift
                peak = high if peak is None else jnp.maximum(peak, high)
            peak = jnp.max(peak, axis=0, keepdims=True) * factor
            weight_sum = jnp.zeros((8, lanes), jnp.float32)
            product_sum = jnp.zeros((8, lanes), jnp.float32)
            for (c, kind), shift in zip(chunks, biases):
                offset = -peak if shift is None else shift * factor - peak
                weights = jnp.exp2(raw(c, kind) * factor + offset)
                scores_at[c * BLK:(c + 1) * BLK, cols] = weights
                weight_sum += folded(weights, jnp.sum)
                product_sum += folded(weights * grad_prob_at[c * BLK:(c + 1) * BLK, cols], jnp.sum)
            inverse = 1.0 / jnp.sum(weight_sum, axis=0, keepdims=True)
            delta = jnp.sum(product_sum, axis=0, keepdims=True) * inverse
            scaled = inverse * jnp.float32(scale)
            for c, kind in chunks:
                at_rows = slice(c * BLK, (c + 1) * BLK)
                weights = scores_at[at_rows, cols]
                probs_at[at_rows, cols] = (weights * inverse).astype(jnp.bfloat16)
                dscore_at[at_rows, cols] = (
                    (weights * scaled) * (grad_prob_at[at_rows, cols] - delta)).astype(jnp.bfloat16)
        dscore = dscore_at[...]
        dquery = jnp.dot(key_p.T, dscore, preferred_element_type=jnp.float32).T
        for half in range(2):
            mine = jnp.concatenate([rows_of(dquery, half * group + h) for h in range(group)], axis=1)
            out_rows = slice(first_row + half * BLK, first_row + (half + 1) * BLK)
            res[t, out_rows, :] = (gr[t, out_rows, :].astype(jnp.float32) + my_gain * mine).astype(jnp.bfloat16)
        for part, term in enumerate((
            jnp.dot(dscore, query_p, preferred_element_type=jnp.float32),
            jnp.dot(probs_at[...], grad_p, preferred_element_type=jnp.float32),
        )):
            if pair == 0:
                acc[t, part, local_rows, :] = term[:PAIR_KEYS * BLK]
                acc[t, part, far_rows, :] = term[PAIR_KEYS * BLK:]
            else:
                seen = (PAIR_KEYS - 2) * BLK
                acc[t, part, first_row:first_row + seen, :] += term[:seen]
                acc[t, part, first_row + seen:first_row + seen + 2 * BLK, :] = term[seen:seen + 2 * BLK]
                acc[t, part, far_rows, :] += term[PAIR_KEYS * BLK:]

    outs = (key_out, value_out)

    def total_out(t, part, k):
        b = lax.rem(me + k, PLANE)
        return pltpu.make_async_remote_copy(
            total.at[t, part, rows_at(b * BLK, BLK), :],
            outs[part].at[0, t, :, columns_at(me * HEAD_DIM, HEAD_DIM)],
            out_send.at[t, part, k], out_recv.at[t, part, me], device_id=at(z, b), device_id_type=MESH)

    def total_in(t, part, k):
        source = lax.rem(me + PLANE - k, PLANE)
        return pltpu.make_async_remote_copy(
            total.at[t, part, rows_at(me * BLK, BLK), :],
            outs[part].at[0, t, :, columns_at(source * HEAD_DIM, HEAD_DIM)],
            out_send.at[t, part, k], out_recv.at[t, part, source], device_id=at(z, source), device_id_type=MESH)

    def total_local(t, part):
        return pltpu.make_async_copy(
            total.at[t, part, rows_at(me * BLK, BLK), :],
            outs[part].at[0, t, :, columns_at(me * HEAD_DIM, HEAD_DIM)], local_sem.at[t, 5 + part])

    def finish(t):
        @pl.when(z + 1 < planes)
        def _():
            near_back(t).wait_recv()
            acc[t, :, OWN:OWN + SPAN, :] += near_in[t].astype(jnp.float32)

        @pl.when(z + 2 < planes)
        def _():
            far_back(t).wait_recv()
            acc[t, :, OWN + SPAN - FAR:OWN + SPAN, :] += far_in[t].astype(jnp.float32)

        def add_strided(q, plane):
            strided_back(t, q, plane).wait_recv()
            acc[t, :, OWN:OWN + BLK, :] += strided_in[t, plane].astype(jnp.float32)

        each_strided(add_strided)
        total[t] = acc[t, :, OWN:OWN + SPAN, :].astype(jnp.bfloat16)
        for part in range(2):
            for k in range(1, PLANE):
                total_out(t, part, k).start()
            total_local(t, part).start()

    send_keys(0)
    for t in range(ticks):
        take_keys(t)
        for pair in range(PLANE // 2):
            blocks = (2 * pair, 2 * pair + 1)
            for b in blocks:
                take_block(t, 2, b)
                if t == 0:
                    take_block(t, 3, b)
                else:
                    pl.when(last)(lambda: take_block(t, 3, b))
                    pl.when(pp < n_pp - 1)(lambda: relay(t - 1, b).wait_recv())
            pair_step(t, pair)
            if t + 1 < ticks:
                for b in blocks:
                    pl.when(pp > 0)(lambda: relay(t, b).start())
            if pair == 0:
                stage[t, :, 0:FAR, :] = acc[t, :, 0:FAR, :].astype(jnp.bfloat16)
                pl.when(z >= 2)(lambda: far_back(t).start())
                if t + 1 < ticks:
                    send_keys(t + 1)
                if t > 0:
                    finish(t - 1)
            for b in blocks:
                pl.when(me != b)(lambda: result_out(t, b).start())
        result_local(t).start()
        stage[t, :, FAR:PREV, :] = acc[t, :, FAR:PREV, :].astype(jnp.bfloat16)
        pl.when(z >= 1)(lambda: near_back(t).start())
        stage[t, :, STRIDED:, :] = acc[t, :, STRIDED:, :].astype(jnp.bfloat16)
        for q in range(owners):
            pl.when(z > step * q)(lambda: strided_back(t, q, z).start())

    finish(ticks - 1)

    for t in range(ticks):
        exchange(t, (0, 1, 2), finish_out)
        exchange(t, (3,), finish_out)
        pl.when(z + 1 < planes)(lambda: near(t).wait_send())
        pl.when(z + 2 < planes)(lambda: far(t).wait_send())
        each_strided(lambda q, plane: strided(t, q, plane).wait_send())
        for b in range(PLANE):
            if t + 1 < ticks:
                pl.when(pp > 0)(lambda: relay(t, b).wait_send())
            pl.when(me != b)(lambda: result_out(t, b).wait_send())
        pl.when(z >= 2)(lambda: far_back(t).wait_send())
        pl.when(z >= 1)(lambda: near_back(t).wait_send())
        for q in range(owners):
            pl.when(z > step * q)(lambda: strided_back(t, q, z).wait_send())
        result_local(t).wait()
        for k in range(1, PLANE):
            result_in(t, lax.rem(me + k, PLANE)).wait_recv()
        for part in range(2):
            total_local(t, part).wait()
            for k in range(1, PLANE):
                total_out(t, part, k).wait_send()
                total_in(t, part, k).wait_recv()


def hand_out(a, b, c, a_out, b_out, c_out, sem):
    copies = [
        pltpu.make_async_copy(src, dst, sem.at[i])
        for i, (src, dst) in enumerate(((a, a_out), (b, b_out), (c, c_out)))
    ]
    for copy in copies:
        copy.start()
    for copy in copies:
        copy.wait()


def body(n_ctx, n_pp, inputs, keys, values, gain, first, head, window, stride):
    ticks = inputs.shape[1]
    feat = inputs.shape[-1]
    kv_heads = keys.shape[-1] // HEAD_DIM
    group = feat // (kv_heads * HEAD_DIM)
    planes = n_ctx // PLANE
    owners = n_ctx // STRIDE
    rows = STRIDED + owners * BLK
    width = group * HEAD_DIM
    bf16, f32 = jnp.bfloat16, jnp.float32
    dma = pltpu.SemaphoreType.DMA
    anywhere = pl.BlockSpec(memory_space=pl.ANY)
    outs = pl.pallas_call(
        functools.partial(kernel, n_ctx, n_pp, ticks, group),
        out_shape=[jax.ShapeDtypeStruct(a.shape, bf16) for a in (inputs, keys, values)],
        in_specs=[pl.BlockSpec(memory_space=pltpu.HBM)] * 8,
        out_specs=[anywhere] * 3,
        scratch_shapes=[
            pltpu.VMEM((ticks, SPAN, width), bf16),
            pltpu.VMEM((ticks, SPAN, width), bf16),
            pltpu.VMEM((ticks, 2, rows, HEAD_DIM), bf16),
            pltpu.VMEM((ticks, SPAN, width), bf16),
            pltpu.VMEM((ticks, 2, rows, HEAD_DIM), f32),
            pltpu.VMEM((ticks, 2, rows, HEAD_DIM), bf16),
            pltpu.VMEM((ticks, 2, SPAN, HEAD_DIM), bf16),
            pltpu.VMEM((ticks, 2, FAR, HEAD_DIM), bf16),
            pltpu.VMEM((ticks, planes, 2, BLK, HEAD_DIM), bf16),
            pltpu.VMEM((ticks, 2, SPAN, HEAD_DIM), bf16),
            pltpu.VMEM(gain.shape, f32), pltpu.SMEM(window.shape, jnp.int32), pltpu.SMEM(stride.shape, jnp.int32),
            dma((3,)),
            pltpu.VMEM(((PAIR_KEYS + owners) * BLK, 2 * group * BLK), f32),
            pltpu.VMEM(((PAIR_KEYS + owners) * BLK, 2 * group * BLK), f32),
            pltpu.VMEM(((PAIR_KEYS + owners) * BLK, 2 * group * BLK), bf16),
            pltpu.VMEM(((PAIR_KEYS + owners) * BLK, 2 * group * BLK), bf16),
            dma((ticks, 7)),
            dma((ticks, 4, PLANE)), dma((ticks, 4, PLANE)),
            dma((ticks, 2)), dma((ticks, 2)),
            dma((ticks, planes)), dma((ticks, owners)),
            dma((ticks, PLANE)), dma((ticks, PLANE)),
            dma((ticks, PLANE)), dma((ticks, PLANE)),
            dma((ticks, 2)), dma((ticks, 2)),
            dma((ticks, owners)), dma((ticks, planes)),
            dma((ticks, 2, PLANE)), dma((ticks, 2, PLANE)),
        ],
        compiler_params=pltpu.CompilerParams(
            collective_id=0, has_side_effects=True, vmem_limit_bytes=40 * 1024 * 1024),
        name="plane_backward",
    )(*[pltpu.with_memory_space_constraint(a, pltpu.HBM) for a in (inputs, keys, values, gain, first, head, window, stride)])
    return pl.pallas_call(
        hand_out,
        out_shape=[jax.ShapeDtypeStruct(a.shape, bf16) for a in (inputs, keys, values)],
        in_specs=[anywhere] * 3,
        out_specs=[pl.BlockSpec(memory_space=pltpu.HBM)] * 3,
        scratch_shapes=[dma((3,))],
        compiler_params=pltpu.CompilerParams(vmem_limit_bytes=40 * 1024 * 1024),
        name="hand_out",
    )(*outs)


def solution(mesh):
    in_specs = (
        P("pp", None, "ctx", None),
        P("pp", None, "ctx", None),
        P("pp", None, "ctx", None),
        P("pp", None),
        P("pp", "ctx", None),
        P(None, "ctx", None),
        P("pp", None),
        P("pp", None),
    )
    out_specs = (P("pp", None, "ctx", None), P("pp", None, "ctx", None), P("pp", None, "ctx", None))
    run = functools.partial(body, mesh.shape["ctx"], mesh.shape["pp"])
    return jax.shard_map(run, mesh=mesh, in_specs=in_specs, out_specs=out_specs, check_vma=False)
```

```python
import functools

import jax
import jax.numpy as jnp
from jax import lax
from jax.experimental import pallas as pl
from jax.experimental.pallas import tpu as pltpu
from jax.sharding import PartitionSpec as P

BLK = 64
WIN = 7
STRIDE = 16
HEAD_DIM = 128
PLANE = 4
SPAN = PLANE * BLK
PREV = (WIN - 1) * BLK
FAR = PREV - SPAN
OWN = PREV
PAIR_KEYS = WIN + 1
STRIDED = PREV + SPAN
MESH = pl.DeviceIdType.MESH
LOG2E = 1.4426950408889634


def rows_at(start, size):
    return pl.ds(pl.multiple_of(start, BLK), size)


def columns_at(start, size):
    return pl.ds(pl.multiple_of(start, HEAD_DIM), size)


def kernel(
    n_ctx, n_pp, ticks, group,
    inputs, keys, values, gain_hbm, first, head, window_hbm, stride_hbm,
    grads_out, key_out, value_out,
    xq, gr, kv, res, acc, stage, near_in, far_in, strided_in, total, gain, window, stride, small_sem,
    scores_at, grad_prob_at, probs_at, dscore_at,
    local_sem, plane_send, plane_recv, z_send, z_recv, str_send, str_recv,
    pass_send, pass_recv, res_send, res_recv,
    back_send, back_recv, sback_send, sback_recv, out_send, out_recv,
):
    planes = n_ctx // PLANE
    owners = n_ctx // STRIDE
    step = STRIDE // PLANE
    width = group * HEAD_DIM
    ctx = lax.axis_index("ctx")
    pp = lax.axis_index("pp")
    z = ctx // PLANE
    me = lax.rem(ctx, PLANE)
    last = pp == n_pp - 1

    def at(plane, place):
        return (plane * PLANE + place, pp)

    barrier = pltpu.get_barrier_semaphore()
    for k in range(1, PLANE):
        pl.semaphore_signal(barrier, inc=1, device_id=at(z, lax.rem(me + k, PLANE)), device_id_type=MESH)
    for k in range(1, planes):
        pl.semaphore_signal(barrier, inc=1, device_id=at(lax.rem(z + k, planes), me), device_id_type=MESH)

    @pl.when(pp > 0)
    def _():
        pl.semaphore_signal(barrier, inc=1, device_id=(ctx, pp - 1), device_id_type=MESH)

    @pl.when(pp < n_pp - 1)
    def _():
        pl.semaphore_signal(barrier, inc=1, device_id=(ctx, pp + 1), device_id_type=MESH)

    def pieces(t, place, source):
        cols = columns_at(place * HEAD_DIM, HEAD_DIM)
        wide = columns_at(place * width, width)
        rows = rows_at(source * BLK, BLK)
        own_rows = rows_at(OWN + source * BLK, BLK)
        grads = first if t == 0 else head
        return (
            (keys.at[0, t, :, cols], kv.at[t, 0, own_rows, :]),
            (values.at[0, t, :, cols], kv.at[t, 1, own_rows, :]),
            (inputs.at[0, t, :, wide], xq.at[t, rows, :]),
            (grads.at[0, :, wide] if t == 0 else grads.at[t - 1, :, wide], gr.at[t, rows, :]),
        )

    def local(t, kind):
        src, dst = pieces(t, me, me)[kind]
        return pltpu.make_async_copy(src, dst, local_sem.at[t, kind])

    def remote(t, kind, k):
        place = lax.rem(me + k, PLANE)
        src, dst = pieces(t, place, me)[kind]
        return pltpu.make_async_remote_copy(
            src, dst, plane_send.at[t, kind, k], plane_recv.at[t, kind, me],
            device_id=at(z, place), device_id_type=MESH)

    def arriving(t, kind, k):
        source = lax.rem(me + PLANE - k, PLANE)
        src, dst = pieces(t, me, source)[kind]
        return pltpu.make_async_remote_copy(
            src, dst, plane_send.at[t, kind, k], plane_recv.at[t, kind, source],
            device_id=at(z, source), device_id_type=MESH)

    def exchange(t, kinds, act):
        def run():
            for kind in kinds:
                act(t, kind)
        if t > 0 and kinds == (3,):
            pl.when(last)(run)
        else:
            run()

    def start(t, kind):
        for k in range(1, PLANE):
            remote(t, kind, k).start()

    def start_local(t, kind):
        local(t, kind).start()

    def finish_in(t, kind):
        local(t, kind).wait()
        for k in range(1, PLANE):
            arriving(t, kind, k).wait_recv()

    def take_block(t, kind, b):
        pl.when(me == b)(lambda: local(t, kind).wait())

        @pl.when(me != b)
        def _():
            src, dst = pieces(t, me, b)[kind]
            pltpu.make_async_remote_copy(
                src, dst, plane_send.at[t, kind, 0], plane_recv.at[t, kind, b],
                device_id=at(z, b), device_id_type=MESH).wait_recv()

    def finish_out(t, kind):
        for k in range(1, PLANE):
            remote(t, kind, k).wait_send()

    small = [
        pltpu.make_async_copy(src, dst, small_sem.at[i])
        for i, (src, dst) in enumerate(((gain_hbm, gain), (window_hbm, window), (stride_hbm, stride)))
    ]
    for copy in small:
        copy.start()
    for t in range(ticks):
        exchange(t, (0, 1, 2), start_local)
        exchange(t, (3,), start_local)

    zero = functools.partial(jnp.zeros, dtype=jnp.bfloat16)

    @pl.when(z == 0)
    def _():
        for t in range(ticks):
            kv[t, :, FAR:PREV, :] = zero((2, SPAN, HEAD_DIM))

    @pl.when(z <= 1)
    def _():
        for t in range(ticks):
            kv[t, :, 0:FAR, :] = zero((2, FAR, HEAD_DIM))

    for q in range(owners):
        @pl.when(z <= step * q)
        def _():
            at_row = STRIDED + q * BLK
            for t in range(ticks):
                kv[t, :, at_row:at_row + BLK, :] = zero((2, BLK, HEAD_DIM))

    probs_at[...] = jnp.zeros_like(probs_at)
    dscore_at[...] = jnp.zeros_like(dscore_at)

    pl.semaphore_wait(
        barrier,
        PLANE - 1 + planes - 1 + jnp.where(pp > 0, 1, 0) + jnp.where(last, 0, 1))

    exchange(0, (0, 1), start)
    exchange(0, (2,), start)
    exchange(0, (3,), start)
    for t in range(1, ticks):
        exchange(t, (0, 1), start)

    def near(t):
        return pltpu.make_async_remote_copy(
            kv.at[t, :, OWN:OWN + SPAN, :], kv.at[t, :, FAR:PREV, :], z_send.at[t, 0], z_recv.at[t, 0],
            device_id=at(z + 1, me), device_id_type=MESH)

    def far(t):
        return pltpu.make_async_remote_copy(
            kv.at[t, :, OWN + SPAN - FAR:OWN + SPAN, :], kv.at[t, :, 0:FAR, :], z_send.at[t, 1], z_recv.at[t, 1],
            device_id=at(z + 2, me), device_id_type=MESH)

    def strided(t, q, plane):
        return pltpu.make_async_remote_copy(
            kv.at[t, :, OWN:OWN + BLK, :], kv.at[t, :, STRIDED + q * BLK:STRIDED + (q + 1) * BLK, :],
            str_send.at[t, plane], str_recv.at[t, q], device_id=at(plane, me), device_id_type=MESH)

    def each_strided(act):
        for q in range(owners):
            @pl.when(z == step * q)
            def _():
                for plane in range(step * q + 1, planes):
                    act(q, plane)

    def send_keys(t):
        exchange(t, (0, 1), finish_in)
        pl.when(z + 1 < planes)(lambda: near(t).start())
        pl.when(z + 2 < planes)(lambda: far(t).start())
        each_strided(lambda q, plane: strided(t, q, plane).start())

    def take_keys(t):
        pl.when(z >= 1)(lambda: near(t).wait_recv())
        pl.when(z >= 2)(lambda: far(t).wait_recv())
        for q in range(owners):
            pl.when(z > step * q)(lambda: strided(t, q, 0).wait_recv())

    def result_out(t, b):
        return pltpu.make_async_remote_copy(
            res.at[t, rows_at(b * BLK, BLK), :], grads_out.at[0, t, :, columns_at(me * width, width)],
            res_send.at[t, b], res_recv.at[t, me], device_id=at(z, b), device_id_type=MESH)

    def result_in(t, source):
        return pltpu.make_async_remote_copy(
            res.at[t, rows_at(me * BLK, BLK), :], grads_out.at[0, t, :, columns_at(source * width, width)],
            res_send.at[t, me], res_recv.at[t, source], device_id=at(z, source), device_id_type=MESH)

    def result_local(t):
        return pltpu.make_async_copy(
            res.at[t, rows_at(me * BLK, BLK), :], grads_out.at[0, t, :, columns_at(me * width, width)],
            local_sem.at[t, 4])

    def relay(t, b):
        rows = rows_at(b * BLK, BLK)
        return pltpu.make_async_remote_copy(
            res.at[t, rows, :], gr.at[t + 1, rows, :], pass_send.at[t, b], pass_recv.at[t, b],
            device_id=(ctx, jnp.maximum(pp - 1, 0)), device_id_type=MESH)

    def near_back(t):
        return pltpu.make_async_remote_copy(
            stage.at[t, :, FAR:PREV, :], near_in.at[t], back_send.at[t, 0], back_recv.at[t, 0],
            device_id=at(z - 1, me), device_id_type=MESH)

    def far_back(t):
        return pltpu.make_async_remote_copy(
            stage.at[t, :, 0:FAR, :], far_in.at[t], back_send.at[t, 1], back_recv.at[t, 1],
            device_id=at(z - 2, me), device_id_type=MESH)

    def strided_back(t, q, plane):
        return pltpu.make_async_remote_copy(
            stage.at[t, :, STRIDED + q * BLK:STRIDED + (q + 1) * BLK, :], strided_in.at[t, plane],
            sback_send.at[t, q], sback_recv.at[t, plane], device_id=at(step * q, me), device_id_type=MESH)

    for copy in small:
        copy.wait()
    my_window = window[0, me]
    my_stride = stride[0, me]
    my_gain = gain[0:1, columns_at(me * width, width)]
    key_ids = lax.broadcasted_iota(jnp.int32, (BLK, group * BLK), 0)
    query_ids = lax.broadcasted_iota(jnp.int32, (BLK, group * BLK), 1) % BLK
    causal = jnp.where(key_ids <= query_ids, jnp.float32(0), jnp.float32(-1e30))
    scale = HEAD_DIM ** -0.5
    contract = (((1,), (1,)), ((), ()))
    rows_of = lambda matrix, c: matrix[c * BLK:(c + 1) * BLK]

    def bias(block, c):
        if c < WIN:
            distance = WIN - 1 - c
            key_block = block - distance
            near_enough = jnp.where(distance < my_window, 1, 0)
            on_stride = jnp.where((key_block & (my_stride - 1)) == 0, 1, 0)
            inside = jnp.where(key_block >= 0, 1, 0)
            allowed = inside * jnp.maximum(near_enough, on_stride)
        else:
            key_block = (c - WIN) * STRIDE
            on_stride = jnp.where((key_block & (my_stride - 1)) == 0, 1, 0)
            allowed = on_stride * jnp.where(key_block <= block - WIN, 1, 0)
        return jnp.where(allowed == 1, jnp.float32(0), jnp.float32(-1e30))

    def stack(matrix):
        return jnp.concatenate([matrix[:, h * HEAD_DIM:(h + 1) * HEAD_DIM] for h in range(group)], axis=0)

    def folded(chunk, combine):
        return combine(chunk.reshape(BLK // 8, 8, lanes), axis=0)

    lanes = group * BLK
    factor = jnp.float32(scale * LOG2E)

    def pair_step(t, pair, send_terms):
        first_row = pair * 2 * BLK
        local_rows = slice(first_row, first_row + PAIR_KEYS * BLK)
        far_rows = slice(STRIDED, STRIDED + owners * BLK)
        key_p = jnp.concatenate([kv[t, 0, local_rows, :], kv[t, 0, far_rows, :]], axis=0)
        value_p = jnp.concatenate([kv[t, 1, local_rows, :], kv[t, 1, far_rows, :]], axis=0)
        rows = slice(first_row, first_row + 2 * BLK)
        queries = (xq[t, rows, :].astype(jnp.float32) * my_gain).astype(jnp.bfloat16)
        grad = gr[t, rows, :]
        query_p = jnp.concatenate([stack(queries[:BLK]), stack(queries[BLK:])], axis=0)
        grad_p = jnp.concatenate([stack(grad[:BLK]), stack(grad[BLK:])], axis=0)
        scores_at[...] = lax.dot_general(key_p, query_p, contract, preferred_element_type=jnp.float32)
        grad_prob_at[...] = lax.dot_general(value_p, grad_p, contract, preferred_element_type=jnp.float32)
        for half in range(2):
            block = z * PLANE + pair * 2 + half
            cols = slice(half * lanes, (half + 1) * lanes)
            chunks = [(c, c - half) for c in range(PAIR_KEYS) if 0 <= c - half < WIN]
            chunks += [(PAIR_KEYS + q, WIN + q) for q in range(owners)]
            biases = [None if kind == WIN - 1 else bias(block, kind) for c, kind in chunks]

            def raw(c, kind):
                chunk = scores_at[c * BLK:(c + 1) * BLK, cols]
                return chunk + causal if kind == WIN - 1 else chunk

            peak = None
            for (c, kind), shift in zip(chunks, biases):
                high = folded(raw(c, kind), jnp.max)
                high = high if shift is None else high + shift
                peak = high if peak is None else jnp.maximum(peak, high)
            peak = jnp.max(peak, axis=0, keepdims=True) * factor
            weight_sum = jnp.zeros((8, lanes), jnp.float32)
            product_sum = jnp.zeros((8, lanes), jnp.float32)
            for (c, kind), shift in zip(chunks, biases):
                offset = -peak if shift is None else shift * factor - peak
                weights = jnp.exp2(raw(c, kind) * factor + offset)
                scores_at[c * BLK:(c + 1) * BLK, cols] = weights
                weight_sum += folded(weights, jnp.sum)
                product_sum += folded(weights * grad_prob_at[c * BLK:(c + 1) * BLK, cols], jnp.sum)
            inverse = 1.0 / jnp.sum(weight_sum, axis=0, keepdims=True)
            delta = jnp.sum(product_sum, axis=0, keepdims=True) * inverse
            scaled = inverse * jnp.float32(scale)
            for c, kind in chunks:
                at_rows = slice(c * BLK, (c + 1) * BLK)
                weights = scores_at[at_rows, cols]
                probs_at[at_rows, cols] = (weights * inverse).astype(jnp.bfloat16)
                dscore_at[at_rows, cols] = (
                    (weights * scaled) * (grad_prob_at[at_rows, cols] - delta)).astype(jnp.bfloat16)
        dscore = dscore_at[...]
        def queries_part():
            dquery = jnp.dot(key_p.T, dscore, preferred_element_type=jnp.float32).T
            for half in range(2):
                mine = jnp.concatenate([rows_of(dquery, half * group + h) for h in range(group)], axis=1)
                out_rows = slice(first_row + half * BLK, first_row + (half + 1) * BLK)
                res[t, out_rows, :] = (gr[t, out_rows, :].astype(jnp.float32) + my_gain * mine).astype(jnp.bfloat16)

        def keys_part():
            for part, term in enumerate((
                jnp.dot(dscore, query_p, preferred_element_type=jnp.float32),
                jnp.dot(probs_at[...], grad_p, preferred_element_type=jnp.float32),
            )):
                if pair == 0:
                    acc[t, part, local_rows, :] = term[:PAIR_KEYS * BLK]
                    acc[t, part, far_rows, :] = term[PAIR_KEYS * BLK:]
                else:
                    seen = (PAIR_KEYS - 2) * BLK
                    acc[t, part, first_row:first_row + seen, :] += term[:seen]
                    acc[t, part, first_row + seen:first_row + seen + 2 * BLK, :] = term[seen:seen + 2 * BLK]
                    acc[t, part, far_rows, :] += term[PAIR_KEYS * BLK:]

        if send_terms is None:
            queries_part()
            keys_part()
        else:
            keys_part()
            send_terms()
            queries_part()

    outs = (key_out, value_out)

    def total_out(t, part, k):
        b = lax.rem(me + k, PLANE)
        return pltpu.make_async_remote_copy(
            total.at[t, part, rows_at(b * BLK, BLK), :],
            outs[part].at[0, t, :, columns_at(me * HEAD_DIM, HEAD_DIM)],
            out_send.at[t, part, k], out_recv.at[t, part, me], device_id=at(z, b), device_id_type=MESH)

    def total_in(t, part, k):
        source = lax.rem(me + PLANE - k, PLANE)
        return pltpu.make_async_remote_copy(
            total.at[t, part, rows_at(me * BLK, BLK), :],
            outs[part].at[0, t, :, columns_at(source * HEAD_DIM, HEAD_DIM)],
            out_send.at[t, part, k], out_recv.at[t, part, source], device_id=at(z, source), device_id_type=MESH)

    def total_local(t, part):
        return pltpu.make_async_copy(
            total.at[t, part, rows_at(me * BLK, BLK), :],
            outs[part].at[0, t, :, columns_at(me * HEAD_DIM, HEAD_DIM)], local_sem.at[t, 5 + part])

    def finish(t):
        @pl.when(z + 1 < planes)
        def _():
            near_back(t).wait_recv()
            acc[t, :, OWN:OWN + SPAN, :] += near_in[t].astype(jnp.float32)

        @pl.when(z + 2 < planes)
        def _():
            far_back(t).wait_recv()
            acc[t, :, OWN + SPAN - FAR:OWN + SPAN, :] += far_in[t].astype(jnp.float32)

        def add_strided(q, plane):
            strided_back(t, q, plane).wait_recv()
            acc[t, :, OWN:OWN + BLK, :] += strided_in[t, plane].astype(jnp.float32)

        each_strided(add_strided)
        total[t] = acc[t, :, OWN:OWN + SPAN, :].astype(jnp.bfloat16)
        for part in range(2):
            for k in range(1, PLANE):
                total_out(t, part, k).start()
            total_local(t, part).start()

    send_keys(0)
    for b in range(PLANE):
        take_block(0, 2, b)
        take_block(0, 3, b)
    for t in range(1, ticks):
        exchange(t, (2,), start)
        exchange(t, (3,), start)
    for t in range(1, ticks):
        send_keys(t)
    for t in range(ticks):
        take_keys(t)
        for pair in range(PLANE // 2):
            blocks = (2 * pair, 2 * pair + 1)
            if t > 0:
                for b in blocks:
                    take_block(t, 2, b)
                    pl.when(last)(lambda: take_block(t, 3, b))
                    pl.when(pp < n_pp - 1)(lambda: relay(t - 1, b).wait_recv())

            def send_terms():
                if pair == 0:
                    stage[t, :, 0:FAR, :] = acc[t, :, 0:FAR, :].astype(jnp.bfloat16)
                    pl.when(z >= 2)(lambda: far_back(t).start())
                else:
                    stage[t, :, FAR:PREV, :] = acc[t, :, FAR:PREV, :].astype(jnp.bfloat16)
                    pl.when(z >= 1)(lambda: near_back(t).start())
                    stage[t, :, STRIDED:, :] = acc[t, :, STRIDED:, :].astype(jnp.bfloat16)
                    for q in range(owners):
                        pl.when(z > step * q)(lambda: strided_back(t, q, z).start())

            pair_step(t, pair, send_terms if t + 1 == ticks else None)
            if t + 1 < ticks:
                for b in blocks:
                    pl.when(pp > 0)(lambda: relay(t, b).start())
                send_terms()
            else:
                for b in blocks:
                    pl.when(me != b)(lambda: result_out(t, b).start())
            if t > 0 and pair == 0:
                finish(t - 1)
        if t + 1 < ticks:
            for b in range(PLANE):
                pl.when(me != b)(lambda: result_out(t, b).start())
        result_local(t).start()
    finish(ticks - 1)

    for t in range(ticks):
        exchange(t, (0, 1, 2), finish_out)
        exchange(t, (3,), finish_out)
        pl.when(z + 1 < planes)(lambda: near(t).wait_send())
        pl.when(z + 2 < planes)(lambda: far(t).wait_send())
        each_strided(lambda q, plane: strided(t, q, plane).wait_send())
        for b in range(PLANE):
            if t + 1 < ticks:
                pl.when(pp > 0)(lambda: relay(t, b).wait_send())
            pl.when(me != b)(lambda: result_out(t, b).wait_send())
        pl.when(z >= 2)(lambda: far_back(t).wait_send())
        pl.when(z >= 1)(lambda: near_back(t).wait_send())
        for q in range(owners):
            pl.when(z > step * q)(lambda: strided_back(t, q, z).wait_send())
        result_local(t).wait()
        for k in range(1, PLANE):
            result_in(t, lax.rem(me + k, PLANE)).wait_recv()
        for part in range(2):
            total_local(t, part).wait()
            for k in range(1, PLANE):
                total_out(t, part, k).wait_send()
                total_in(t, part, k).wait_recv()


def hand_out(a, b, c, a_out, b_out, c_out, sem):
    copies = [
        pltpu.make_async_copy(src, dst, sem.at[i])
        for i, (src, dst) in enumerate(((a, a_out), (b, b_out), (c, c_out)))
    ]
    for copy in copies:
        copy.start()
    for copy in copies:
        copy.wait()


def body(n_ctx, n_pp, inputs, keys, values, gain, first, head, window, stride):
    ticks = inputs.shape[1]
    feat = inputs.shape[-1]
    kv_heads = keys.shape[-1] // HEAD_DIM
    group = feat // (kv_heads * HEAD_DIM)
    planes = n_ctx // PLANE
    owners = n_ctx // STRIDE
    rows = STRIDED + owners * BLK
    width = group * HEAD_DIM
    bf16, f32 = jnp.bfloat16, jnp.float32
    dma = pltpu.SemaphoreType.DMA
    anywhere = pl.BlockSpec(memory_space=pl.ANY)
    outs = pl.pallas_call(
        functools.partial(kernel, n_ctx, n_pp, ticks, group),
        out_shape=[jax.ShapeDtypeStruct(a.shape, bf16) for a in (inputs, keys, values)],
        in_specs=[pl.BlockSpec(memory_space=pltpu.HBM)] * 8,
        out_specs=[anywhere] * 3,
        scratch_shapes=[
            pltpu.VMEM((ticks, SPAN, width), bf16),
            pltpu.VMEM((ticks, SPAN, width), bf16),
            pltpu.VMEM((ticks, 2, rows, HEAD_DIM), bf16),
            pltpu.VMEM((ticks, SPAN, width), bf16),
            pltpu.VMEM((ticks, 2, rows, HEAD_DIM), f32),
            pltpu.VMEM((ticks, 2, rows, HEAD_DIM), bf16),
            pltpu.VMEM((ticks, 2, SPAN, HEAD_DIM), bf16),
            pltpu.VMEM((ticks, 2, FAR, HEAD_DIM), bf16),
            pltpu.VMEM((ticks, planes, 2, BLK, HEAD_DIM), bf16),
            pltpu.VMEM((ticks, 2, SPAN, HEAD_DIM), bf16),
            pltpu.VMEM(gain.shape, f32), pltpu.SMEM(window.shape, jnp.int32), pltpu.SMEM(stride.shape, jnp.int32),
            dma((3,)),
            pltpu.VMEM(((PAIR_KEYS + owners) * BLK, 2 * group * BLK), f32),
            pltpu.VMEM(((PAIR_KEYS + owners) * BLK, 2 * group * BLK), f32),
            pltpu.VMEM(((PAIR_KEYS + owners) * BLK, 2 * group * BLK), bf16),
            pltpu.VMEM(((PAIR_KEYS + owners) * BLK, 2 * group * BLK), bf16),
            dma((ticks, 7)),
            dma((ticks, 4, PLANE)), dma((ticks, 4, PLANE)),
            dma((ticks, 2)), dma((ticks, 2)),
            dma((ticks, planes)), dma((ticks, owners)),
            dma((ticks, PLANE)), dma((ticks, PLANE)),
            dma((ticks, PLANE)), dma((ticks, PLANE)),
            dma((ticks, 2)), dma((ticks, 2)),
            dma((ticks, owners)), dma((ticks, planes)),
            dma((ticks, 2, PLANE)), dma((ticks, 2, PLANE)),
        ],
        compiler_params=pltpu.CompilerParams(
            collective_id=0, has_side_effects=True, vmem_limit_bytes=40 * 1024 * 1024),
        name="plane_backward",
    )(*[pltpu.with_memory_space_constraint(a, pltpu.HBM) for a in (inputs, keys, values, gain, first, head, window, stride)])
    return pl.pallas_call(
        hand_out,
        out_shape=[jax.ShapeDtypeStruct(a.shape, bf16) for a in (inputs, keys, values)],
        in_specs=[anywhere] * 3,
        out_specs=[pl.BlockSpec(memory_space=pltpu.HBM)] * 3,
        scratch_shapes=[dma((3,))],
        compiler_params=pltpu.CompilerParams(vmem_limit_bytes=40 * 1024 * 1024),
        name="hand_out",
    )(*outs)


def solution(mesh):
    in_specs = (
        P("pp", None, "ctx", None),
        P("pp", None, "ctx", None),
        P("pp", None, "ctx", None),
        P("pp", None),
        P("pp", "ctx", None),
        P(None, "ctx", None),
        P("pp", None),
        P("pp", None),
    )
    out_specs = (P("pp", None, "ctx", None), P("pp", None, "ctx", None), P("pp", None, "ctx", None))
    run = functools.partial(body, mesh.shape["ctx"], mesh.shape["pp"])
    return jax.shard_map(run, mesh=mesh, in_specs=in_specs, out_specs=out_specs, check_vma=False)
```

```python
import functools

import jax
import jax.numpy as jnp
from jax import lax
from jax.experimental import pallas as pl
from jax.experimental.pallas import tpu as pltpu
from jax.sharding import PartitionSpec as P

BLK = 64
WIN = 7
STRIDE = 16
HEAD_DIM = 128
PLANE = 4
SPAN = PLANE * BLK
PREV = (WIN - 1) * BLK
FAR = PREV - SPAN
OWN = PREV
PAIR_KEYS = WIN + 1
STRIDED = PREV + SPAN
MESH = pl.DeviceIdType.MESH
LOG2E = 1.4426950408889634


def rows_at(start, size):
    return pl.ds(pl.multiple_of(start, BLK), size)


def columns_at(start, size):
    return pl.ds(pl.multiple_of(start, HEAD_DIM), size)


def kernel(
    n_ctx, n_pp, ticks, group,
    inputs, keys, values, gain_hbm, first, head, window_hbm, stride_hbm,
    grads_out, key_out, value_out,
    xq, gr, kv, res, acc, stage, near_in, far_in, strided_in, total, gain, window, stride, small_sem,
    scores_at, grad_prob_at, probs_at, dscore_at,
    local_sem, plane_send, plane_recv, z_send, z_recv, str_send, str_recv,
    pass_send, pass_recv, res_send, res_recv,
    back_send, back_recv, sback_send, sback_recv, out_send, out_recv,
):
    planes = n_ctx // PLANE
    owners = n_ctx // STRIDE
    step = STRIDE // PLANE
    width = group * HEAD_DIM
    ctx = lax.axis_index("ctx")
    pp = lax.axis_index("pp")
    z = ctx // PLANE
    me = lax.rem(ctx, PLANE)
    last = pp == n_pp - 1

    def at(plane, place):
        return (plane * PLANE + place, pp)

    barrier = pltpu.get_barrier_semaphore()
    for k in range(1, PLANE):
        pl.semaphore_signal(barrier, inc=1, device_id=at(z, lax.rem(me + k, PLANE)), device_id_type=MESH)
    for k in range(1, planes):
        pl.semaphore_signal(barrier, inc=1, device_id=at(lax.rem(z + k, planes), me), device_id_type=MESH)

    @pl.when(pp > 0)
    def _():
        pl.semaphore_signal(barrier, inc=1, device_id=(ctx, pp - 1), device_id_type=MESH)

    @pl.when(pp < n_pp - 1)
    def _():
        pl.semaphore_signal(barrier, inc=1, device_id=(ctx, pp + 1), device_id_type=MESH)

    def pieces(t, place, source):
        cols = columns_at(place * HEAD_DIM, HEAD_DIM)
        wide = columns_at(place * width, width)
        rows = rows_at(source * BLK, BLK)
        own_rows = rows_at(OWN + source * BLK, BLK)
        grads = first if t == 0 else head
        return (
            (keys.at[0, t, :, cols], kv.at[t, 0, own_rows, :]),
            (values.at[0, t, :, cols], kv.at[t, 1, own_rows, :]),
            (inputs.at[0, t, :, wide], xq.at[t, rows, :]),
            (grads.at[0, :, wide] if t == 0 else grads.at[t - 1, :, wide], gr.at[t, rows, :]),
        )

    def local(t, kind):
        src, dst = pieces(t, me, me)[kind]
        return pltpu.make_async_copy(src, dst, local_sem.at[t, kind])

    def remote(t, kind, k):
        place = lax.rem(me + k, PLANE)
        src, dst = pieces(t, place, me)[kind]
        return pltpu.make_async_remote_copy(
            src, dst, plane_send.at[t, kind, k], plane_recv.at[t, kind, me],
            device_id=at(z, place), device_id_type=MESH)

    def arriving(t, kind, k):
        source = lax.rem(me + PLANE - k, PLANE)
        src, dst = pieces(t, me, source)[kind]
        return pltpu.make_async_remote_copy(
            src, dst, plane_send.at[t, kind, k], plane_recv.at[t, kind, source],
            device_id=at(z, source), device_id_type=MESH)

    def exchange(t, kinds, act):
        def run():
            for kind in kinds:
                act(t, kind)
        if t > 0 and kinds == (3,):
            pl.when(last)(run)
        else:
            run()

    def start(t, kind):
        for k in range(1, PLANE):
            remote(t, kind, k).start()

    def start_local(t, kind):
        local(t, kind).start()

    def finish_in(t, kind):
        local(t, kind).wait()
        for k in range(1, PLANE):
            arriving(t, kind, k).wait_recv()

    def take_block(t, kind, b):
        pl.when(me == b)(lambda: local(t, kind).wait())

        @pl.when(me != b)
        def _():
            src, dst = pieces(t, me, b)[kind]
            pltpu.make_async_remote_copy(
                src, dst, plane_send.at[t, kind, 0], plane_recv.at[t, kind, b],
                device_id=at(z, b), device_id_type=MESH).wait_recv()

    def finish_out(t, kind):
        for k in range(1, PLANE):
            remote(t, kind, k).wait_send()

    small = [
        pltpu.make_async_copy(src, dst, small_sem.at[i])
        for i, (src, dst) in enumerate(((gain_hbm, gain), (window_hbm, window), (stride_hbm, stride)))
    ]
    for copy in small:
        copy.start()
    for t in range(ticks):
        exchange(t, (0, 1, 2), start_local)
        exchange(t, (3,), start_local)

    zero = functools.partial(jnp.zeros, dtype=jnp.bfloat16)

    @pl.when(z == 0)
    def _():
        for t in range(ticks):
            kv[t, :, FAR:PREV, :] = zero((2, SPAN, HEAD_DIM))

    @pl.when(z <= 1)
    def _():
        for t in range(ticks):
            kv[t, :, 0:FAR, :] = zero((2, FAR, HEAD_DIM))

    for q in range(owners):
        @pl.when(z <= step * q)
        def _():
            at_row = STRIDED + q * BLK
            for t in range(ticks):
                kv[t, :, at_row:at_row + BLK, :] = zero((2, BLK, HEAD_DIM))

    probs_at[...] = jnp.zeros_like(probs_at)
    dscore_at[...] = jnp.zeros_like(dscore_at)

    pl.semaphore_wait(
        barrier,
        PLANE - 1 + planes - 1 + jnp.where(pp > 0, 1, 0) + jnp.where(last, 0, 1))

    exchange(0, (0, 1), start)
    exchange(0, (2,), start)
    exchange(0, (3,), start)
    for t in range(1, ticks):
        exchange(t, (0, 1), start)

    def near(t):
        return pltpu.make_async_remote_copy(
            kv.at[t, :, OWN:OWN + SPAN, :], kv.at[t, :, FAR:PREV, :], z_send.at[t, 0], z_recv.at[t, 0],
            device_id=at(z + 1, me), device_id_type=MESH)

    def far(t):
        return pltpu.make_async_remote_copy(
            kv.at[t, :, PREV - FAR:PREV, :], kv.at[t, :, 0:FAR, :], z_send.at[t, 1], z_recv.at[t, 1],
            device_id=at(z + 1, me), device_id_type=MESH)

    def strided(t, q, plane):
        return pltpu.make_async_remote_copy(
            kv.at[t, :, OWN:OWN + BLK, :], kv.at[t, :, STRIDED + q * BLK:STRIDED + (q + 1) * BLK, :],
            str_send.at[t, plane], str_recv.at[t, q], device_id=at(plane, me), device_id_type=MESH)

    def each_strided(act):
        for q in range(owners):
            @pl.when(z == step * q)
            def _():
                for plane in range(step * q + 2, planes):
                    act(q, plane)

    def send_keys(t):
        exchange(t, (0, 1), finish_in)
        pl.when(z + 1 < planes)(lambda: near(t).start())
        each_strided(lambda q, plane: strided(t, q, plane).start())

    def pass_keys(t):
        pl.when(z >= 1)(lambda: near(t).wait_recv())
        pl.when((z >= 1) & (z + 1 < planes))(lambda: far(t).start())
        for q in range(owners):
            @pl.when(z == step * q + 1)
            def _():
                kv[t, :, STRIDED + q * BLK:STRIDED + (q + 1) * BLK, :] = kv[t, :, FAR:FAR + BLK, :]

    def take_keys(t):
        pl.when(z >= 2)(lambda: far(t).wait_recv())
        for q in range(owners):
            pl.when(z > step * q + 1)(lambda: strided(t, q, 0).wait_recv())

    def result_out(t, b):
        return pltpu.make_async_remote_copy(
            res.at[t, rows_at(b * BLK, BLK), :], grads_out.at[0, t, :, columns_at(me * width, width)],
            res_send.at[t, b], res_recv.at[t, me], device_id=at(z, b), device_id_type=MESH)

    def result_in(t, source):
        return pltpu.make_async_remote_copy(
            res.at[t, rows_at(me * BLK, BLK), :], grads_out.at[0, t, :, columns_at(source * width, width)],
            res_send.at[t, me], res_recv.at[t, source], device_id=at(z, source), device_id_type=MESH)

    def result_local(t):
        return pltpu.make_async_copy(
            res.at[t, rows_at(me * BLK, BLK), :], grads_out.at[0, t, :, columns_at(me * width, width)],
            local_sem.at[t, 4])

    def relay(t, b):
        rows = rows_at(b * BLK, BLK)
        return pltpu.make_async_remote_copy(
            res.at[t, rows, :], gr.at[t + 1, rows, :], pass_send.at[t, b], pass_recv.at[t, b],
            device_id=(ctx, jnp.maximum(pp - 1, 0)), device_id_type=MESH)

    def near_back(t):
        return pltpu.make_async_remote_copy(
            stage.at[t, :, FAR:PREV, :], near_in.at[t], back_send.at[t, 0], back_recv.at[t, 0],
            device_id=at(z - 1, me), device_id_type=MESH)

    def far_back(t):
        return pltpu.make_async_remote_copy(
            stage.at[t, :, 0:FAR, :], far_in.at[t], back_send.at[t, 1], back_recv.at[t, 1],
            device_id=at(z - 1, me), device_id_type=MESH)

    def strided_back(t, q, plane):
        return pltpu.make_async_remote_copy(
            stage.at[t, :, STRIDED + q * BLK:STRIDED + (q + 1) * BLK, :], strided_in.at[t, plane],
            sback_send.at[t, q], sback_recv.at[t, plane], device_id=at(step * q, me), device_id_type=MESH)

    for copy in small:
        copy.wait()
    my_window = window[0, me]
    my_stride = stride[0, me]
    my_gain = gain[0:1, columns_at(me * width, width)]
    key_ids = lax.broadcasted_iota(jnp.int32, (BLK, group * BLK), 0)
    query_ids = lax.broadcasted_iota(jnp.int32, (BLK, group * BLK), 1) % BLK
    causal = jnp.where(key_ids <= query_ids, jnp.float32(0), jnp.float32(-1e30))
    scale = HEAD_DIM ** -0.5
    contract = (((1,), (1,)), ((), ()))
    rows_of = lambda matrix, c: matrix[c * BLK:(c + 1) * BLK]

    def bias(block, c):
        if c < WIN:
            distance = WIN - 1 - c
            key_block = block - distance
            near_enough = jnp.where(distance < my_window, 1, 0)
            on_stride = jnp.where((key_block & (my_stride - 1)) == 0, 1, 0)
            inside = jnp.where(key_block >= 0, 1, 0)
            allowed = inside * jnp.maximum(near_enough, on_stride)
        else:
            key_block = (c - WIN) * STRIDE
            on_stride = jnp.where((key_block & (my_stride - 1)) == 0, 1, 0)
            allowed = on_stride * jnp.where(key_block <= block - WIN, 1, 0)
        return jnp.where(allowed == 1, jnp.float32(0), jnp.float32(-1e30))

    def stack(matrix):
        return jnp.concatenate([matrix[:, h * HEAD_DIM:(h + 1) * HEAD_DIM] for h in range(group)], axis=0)

    def folded(chunk, combine):
        return combine(chunk.reshape(BLK // 8, 8, lanes), axis=0)

    lanes = group * BLK
    factor = jnp.float32(scale * LOG2E)

    def pair_step(t, pair, send_terms):
        first_row = pair * 2 * BLK
        local_rows = slice(first_row, first_row + PAIR_KEYS * BLK)
        far_rows = slice(STRIDED, STRIDED + owners * BLK)
        key_p = jnp.concatenate([kv[t, 0, local_rows, :], kv[t, 0, far_rows, :]], axis=0)
        value_p = jnp.concatenate([kv[t, 1, local_rows, :], kv[t, 1, far_rows, :]], axis=0)
        rows = slice(first_row, first_row + 2 * BLK)
        queries = (xq[t, rows, :].astype(jnp.float32) * my_gain).astype(jnp.bfloat16)
        grad = gr[t, rows, :]
        query_p = jnp.concatenate([stack(queries[:BLK]), stack(queries[BLK:])], axis=0)
        grad_p = jnp.concatenate([stack(grad[:BLK]), stack(grad[BLK:])], axis=0)
        scores_at[...] = lax.dot_general(key_p, query_p, contract, preferred_element_type=jnp.float32)
        grad_prob_at[...] = lax.dot_general(value_p, grad_p, contract, preferred_element_type=jnp.float32)
        for half in range(2):
            block = z * PLANE + pair * 2 + half
            cols = slice(half * lanes, (half + 1) * lanes)
            chunks = [(c, c - half) for c in range(PAIR_KEYS) if 0 <= c - half < WIN]
            chunks += [(PAIR_KEYS + q, WIN + q) for q in range(owners)]
            biases = [None if kind == WIN - 1 else bias(block, kind) for c, kind in chunks]

            def raw(c, kind):
                chunk = scores_at[c * BLK:(c + 1) * BLK, cols]
                return chunk + causal if kind == WIN - 1 else chunk

            peak = None
            for (c, kind), shift in zip(chunks, biases):
                high = folded(raw(c, kind), jnp.max)
                high = high if shift is None else high + shift
                peak = high if peak is None else jnp.maximum(peak, high)
            peak = jnp.max(peak, axis=0, keepdims=True) * factor
            weight_sum = jnp.zeros((8, lanes), jnp.float32)
            product_sum = jnp.zeros((8, lanes), jnp.float32)
            for (c, kind), shift in zip(chunks, biases):
                offset = -peak if shift is None else shift * factor - peak
                weights = jnp.exp2(raw(c, kind) * factor + offset)
                scores_at[c * BLK:(c + 1) * BLK, cols] = weights
                weight_sum += folded(weights, jnp.sum)
                product_sum += folded(weights * grad_prob_at[c * BLK:(c + 1) * BLK, cols], jnp.sum)
            inverse = 1.0 / jnp.sum(weight_sum, axis=0, keepdims=True)
            delta = jnp.sum(product_sum, axis=0, keepdims=True) * inverse
            scaled = inverse * jnp.float32(scale)
            for c, kind in chunks:
                at_rows = slice(c * BLK, (c + 1) * BLK)
                weights = scores_at[at_rows, cols]
                probs_at[at_rows, cols] = (weights * inverse).astype(jnp.bfloat16)
                dscore_at[at_rows, cols] = (
                    (weights * scaled) * (grad_prob_at[at_rows, cols] - delta)).astype(jnp.bfloat16)
        dscore = dscore_at[...]
        def queries_part():
            dquery = jnp.dot(key_p.T, dscore, preferred_element_type=jnp.float32).T
            for half in range(2):
                mine = jnp.concatenate([rows_of(dquery, half * group + h) for h in range(group)], axis=1)
                out_rows = slice(first_row + half * BLK, first_row + (half + 1) * BLK)
                res[t, out_rows, :] = (gr[t, out_rows, :].astype(jnp.float32) + my_gain * mine).astype(jnp.bfloat16)

        def keys_part():
            for part, term in enumerate((
                jnp.dot(dscore, query_p, preferred_element_type=jnp.float32),
                jnp.dot(probs_at[...], grad_p, preferred_element_type=jnp.float32),
            )):
                if pair == 0:
                    acc[t, part, local_rows, :] = term[:PAIR_KEYS * BLK]
                    acc[t, part, far_rows, :] = term[PAIR_KEYS * BLK:]
                else:
                    seen = (PAIR_KEYS - 2) * BLK
                    acc[t, part, first_row:first_row + seen, :] += term[:seen]
                    acc[t, part, first_row + seen:first_row + seen + 2 * BLK, :] = term[seen:seen + 2 * BLK]
                    acc[t, part, far_rows, :] += term[PAIR_KEYS * BLK:]

        if send_terms is None:
            queries_part()
            keys_part()
        else:
            keys_part()
            send_terms()
            queries_part()

    outs = (key_out, value_out)

    def total_out(t, part, k):
        b = lax.rem(me + k, PLANE)
        return pltpu.make_async_remote_copy(
            total.at[t, part, rows_at(b * BLK, BLK), :],
            outs[part].at[0, t, :, columns_at(me * HEAD_DIM, HEAD_DIM)],
            out_send.at[t, part, k], out_recv.at[t, part, me], device_id=at(z, b), device_id_type=MESH)

    def total_in(t, part, k):
        source = lax.rem(me + PLANE - k, PLANE)
        return pltpu.make_async_remote_copy(
            total.at[t, part, rows_at(me * BLK, BLK), :],
            outs[part].at[0, t, :, columns_at(source * HEAD_DIM, HEAD_DIM)],
            out_send.at[t, part, k], out_recv.at[t, part, source], device_id=at(z, source), device_id_type=MESH)

    def total_local(t, part):
        return pltpu.make_async_copy(
            total.at[t, part, rows_at(me * BLK, BLK), :],
            outs[part].at[0, t, :, columns_at(me * HEAD_DIM, HEAD_DIM)], local_sem.at[t, 5 + part])

    def finish(t):
        @pl.when(z + 1 < planes)
        def _():
            near_back(t).wait_recv()
            acc[t, :, OWN:OWN + SPAN, :] += near_in[t].astype(jnp.float32)

        def add_strided(q, plane):
            strided_back(t, q, plane).wait_recv()
            acc[t, :, OWN:OWN + BLK, :] += strided_in[t, plane].astype(jnp.float32)

        each_strided(add_strided)
        total[t] = acc[t, :, OWN:OWN + SPAN, :].astype(jnp.bfloat16)
        for part in range(2):
            for k in range(1, PLANE):
                total_out(t, part, k).start()
            total_local(t, part).start()

    send_keys(0)
    pass_keys(0)
    for b in range(PLANE):
        take_block(0, 2, b)
        take_block(0, 3, b)
    for t in range(1, ticks):
        exchange(t, (2,), start)
        exchange(t, (3,), start)
    for t in range(1, ticks):
        send_keys(t)
    for t in range(ticks):
        take_keys(t)
        for pair in range(PLANE // 2):
            blocks = (2 * pair, 2 * pair + 1)
            if t > 0:
                for b in blocks:
                    take_block(t, 2, b)
                    pl.when(last)(lambda: take_block(t, 3, b))
                    pl.when(pp < n_pp - 1)(lambda: relay(t - 1, b).wait_recv())

            def send_terms():
                if pair == 0:
                    stage[t, :, 0:FAR, :] = acc[t, :, 0:FAR, :].astype(jnp.bfloat16)
                    pl.when(z >= 2)(lambda: far_back(t).start())
                else:
                    @pl.when((z >= 1) & (z + 1 < planes))
                    def _():
                        far_back(t).wait_recv()
                        acc[t, :, PREV - FAR:PREV, :] += far_in[t].astype(jnp.float32)

                    for q in range(owners):
                        @pl.when(z == step * q + 1)
                        def _():
                            slot = STRIDED + q * BLK
                            acc[t, :, FAR:FAR + BLK, :] += acc[t, :, slot:slot + BLK, :]

                    stage[t, :, FAR:PREV, :] = acc[t, :, FAR:PREV, :].astype(jnp.bfloat16)
                    pl.when(z >= 1)(lambda: near_back(t).start())
                    stage[t, :, STRIDED:, :] = acc[t, :, STRIDED:, :].astype(jnp.bfloat16)
                    for q in range(owners):
                        pl.when(z > step * q + 1)(lambda: strided_back(t, q, z).start())

            pair_step(t, pair, send_terms if t + 1 == ticks else None)
            if t + 1 < ticks:
                for b in blocks:
                    pl.when(pp > 0)(lambda: relay(t, b).start())
                send_terms()
                if pair == 0:
                    pass_keys(t + 1)
            else:
                for b in blocks:
                    pl.when(me != b)(lambda: result_out(t, b).start())
            if t > 0 and pair == 0:
                finish(t - 1)
        if t + 1 < ticks:
            for b in range(PLANE):
                pl.when(me != b)(lambda: result_out(t, b).start())
        result_local(t).start()
    finish(ticks - 1)

    for t in range(ticks):
        exchange(t, (0, 1, 2), finish_out)
        exchange(t, (3,), finish_out)
        pl.when(z + 1 < planes)(lambda: near(t).wait_send())
        pl.when((z >= 1) & (z + 1 < planes))(lambda: far(t).wait_send())
        each_strided(lambda q, plane: strided(t, q, plane).wait_send())
        for b in range(PLANE):
            if t + 1 < ticks:
                pl.when(pp > 0)(lambda: relay(t, b).wait_send())
            pl.when(me != b)(lambda: result_out(t, b).wait_send())
        pl.when(z >= 2)(lambda: far_back(t).wait_send())
        pl.when(z >= 1)(lambda: near_back(t).wait_send())
        for q in range(owners):
            pl.when(z > step * q + 1)(lambda: strided_back(t, q, z).wait_send())
        result_local(t).wait()
        for k in range(1, PLANE):
            result_in(t, lax.rem(me + k, PLANE)).wait_recv()
        for part in range(2):
            total_local(t, part).wait()
            for k in range(1, PLANE):
                total_out(t, part, k).wait_send()
                total_in(t, part, k).wait_recv()


def hand_out(a, b, c, a_out, b_out, c_out, sem):
    copies = [
        pltpu.make_async_copy(src, dst, sem.at[i])
        for i, (src, dst) in enumerate(((a, a_out), (b, b_out), (c, c_out)))
    ]
    for copy in copies:
        copy.start()
    for copy in copies:
        copy.wait()


def body(n_ctx, n_pp, inputs, keys, values, gain, first, head, window, stride):
    ticks = inputs.shape[1]
    feat = inputs.shape[-1]
    kv_heads = keys.shape[-1] // HEAD_DIM
    group = feat // (kv_heads * HEAD_DIM)
    planes = n_ctx // PLANE
    owners = n_ctx // STRIDE
    rows = STRIDED + owners * BLK
    width = group * HEAD_DIM
    bf16, f32 = jnp.bfloat16, jnp.float32
    dma = pltpu.SemaphoreType.DMA
    anywhere = pl.BlockSpec(memory_space=pl.ANY)
    outs = pl.pallas_call(
        functools.partial(kernel, n_ctx, n_pp, ticks, group),
        out_shape=[jax.ShapeDtypeStruct(a.shape, bf16) for a in (inputs, keys, values)],
        in_specs=[pl.BlockSpec(memory_space=pltpu.HBM)] * 8,
        out_specs=[anywhere] * 3,
        scratch_shapes=[
            pltpu.VMEM((ticks, SPAN, width), bf16),
            pltpu.VMEM((ticks, SPAN, width), bf16),
            pltpu.VMEM((ticks, 2, rows, HEAD_DIM), bf16),
            pltpu.VMEM((ticks, SPAN, width), bf16),
            pltpu.VMEM((ticks, 2, rows, HEAD_DIM), f32),
            pltpu.VMEM((ticks, 2, rows, HEAD_DIM), bf16),
            pltpu.VMEM((ticks, 2, SPAN, HEAD_DIM), bf16),
            pltpu.VMEM((ticks, 2, FAR, HEAD_DIM), bf16),
            pltpu.VMEM((ticks, planes, 2, BLK, HEAD_DIM), bf16),
            pltpu.VMEM((ticks, 2, SPAN, HEAD_DIM), bf16),
            pltpu.VMEM(gain.shape, f32), pltpu.SMEM(window.shape, jnp.int32), pltpu.SMEM(stride.shape, jnp.int32),
            dma((3,)),
            pltpu.VMEM(((PAIR_KEYS + owners) * BLK, 2 * group * BLK), f32),
            pltpu.VMEM(((PAIR_KEYS + owners) * BLK, 2 * group * BLK), f32),
            pltpu.VMEM(((PAIR_KEYS + owners) * BLK, 2 * group * BLK), bf16),
            pltpu.VMEM(((PAIR_KEYS + owners) * BLK, 2 * group * BLK), bf16),
            dma((ticks, 7)),
            dma((ticks, 4, PLANE)), dma((ticks, 4, PLANE)),
            dma((ticks, 2)), dma((ticks, 2)),
            dma((ticks, planes)), dma((ticks, owners)),
            dma((ticks, PLANE)), dma((ticks, PLANE)),
            dma((ticks, PLANE)), dma((ticks, PLANE)),
            dma((ticks, 2)), dma((ticks, 2)),
            dma((ticks, owners)), dma((ticks, planes)),
            dma((ticks, 2, PLANE)), dma((ticks, 2, PLANE)),
        ],
        compiler_params=pltpu.CompilerParams(
            collective_id=0, has_side_effects=True, vmem_limit_bytes=40 * 1024 * 1024),
        name="plane_backward",
    )(*[pltpu.with_memory_space_constraint(a, pltpu.HBM) for a in (inputs, keys, values, gain, first, head, window, stride)])
    return pl.pallas_call(
        hand_out,
        out_shape=[jax.ShapeDtypeStruct(a.shape, bf16) for a in (inputs, keys, values)],
        in_specs=[anywhere] * 3,
        out_specs=[pl.BlockSpec(memory_space=pltpu.HBM)] * 3,
        scratch_shapes=[dma((3,))],
        compiler_params=pltpu.CompilerParams(vmem_limit_bytes=40 * 1024 * 1024),
        name="hand_out",
    )(*outs)


def solution(mesh):
    in_specs = (
        P("pp", None, "ctx", None),
        P("pp", None, "ctx", None),
        P("pp", None, "ctx", None),
        P("pp", None),
        P("pp", "ctx", None),
        P(None, "ctx", None),
        P("pp", None),
        P("pp", None),
    )
    out_specs = (P("pp", None, "ctx", None), P("pp", None, "ctx", None), P("pp", None, "ctx", None))
    run = functools.partial(body, mesh.shape["ctx"], mesh.shape["pp"])
    return jax.shard_map(run, mesh=mesh, in_specs=in_specs, out_specs=out_specs, check_vma=False)
```
